512 devices in a mesh: dp: 32 (over y, z_hi, core), ctx: 16 (over z_lo, x).
Axes of the slice: x: 4, y: 4, z: 16 (z_hi: 4, z_lo: 4; z = z_hi * 4 + z_lo), core: 2. Of those that a mesh axis runs over, the one named last changes fastest.
Arguments:
- q_lin: bfloat16 [32, 2048, 1792], P('dp', 'ctx'), may hold values from -100 to 100
- k_lin: bfloat16 [32, 2048, 256], P('dp', 'ctx'), may hold values from -12 to 12
- v_lin: bfloat16 [32, 2048, 256], P('dp', 'ctx'), may hold values from -6 to 6
- out_grad: bfloat16 [32, 2048, 1792], P('dp', 'ctx'), may hold values from -6 to 6
- q_bias: float32 [1792], replicated, may hold values from -3 to 3
- doc_lengths: int32 [32, 16], P('dp'), may hold values from 1 to 1152, 2048 in all within a row
Outputs:
- attended: bfloat16 [32, 2048, 1792], P('dp', 'ctx')
- grad_q: bfloat16 [32, 2048, 1792], P('dp', 'ctx')
- grad_k: bfloat16 [32, 2048, 256], P('dp', 'ctx')
- grad_v: bfloat16 [32, 2048, 256], P('dp', 'ctx')
- bias_grad: float32 [1792], replicated
The draws below stay inside these ranges and needn't reach their ends.
Inputs may be any that keep to these rules, and one draw needn't show every extreme that they name: `doc_lengths`: each row holds 16 document lengths that sum to 2048; the longest is exactly 1152.
All inputs are finite; a program needn't handle non-finite values.
Results may differ from the reference program's by a relative error of at most 0.025.
The reference program's roundings to bfloat16 on the way (of `queries`, `rotated_keys`, `weights` and `dscore`) count: a program that leaves them out, or rounds other values in their place, can miss the bound.
Values may be sent and summed in bfloat16 or wider, within the bound.
A program may use at most 64 MiB of HBM per device.

```python
import math
import jax
import jax.numpy as jnp
import numpy as np
from jax import lax

HQ = 14
HK = 2
HD = 128
DOCS = 16
SEQ = 2048
LONGEST = 1152
BATCH = 32
N_CTX = 16


def draw_q_lin(key, part):
    own_key = jax.random.fold_in(key, 1)
    shape = (BATCH, SEQ, HQ * HD)
    return jnp.clip(jax.random.normal(own_key, shape, jnp.float32), -6.0, 6.0).astype(jnp.bfloat16)


def draw_k_lin(key, part):
    own_key = jax.random.fold_in(key, 2)
    shape = (BATCH, SEQ, HK * HD)
    return jnp.clip(jax.random.normal(own_key, shape, jnp.float32), -6.0, 6.0).astype(jnp.bfloat16)


def shard_levels(key, shape, pieces, least, top_value):
    loudness, own = 1.0, jax.random.fold_in(key, 6)
    for axis_at, shards_of in pieces:
        draws = jnp.exp(jax.random.uniform(jax.random.fold_in(own, axis_at), (shards_of,), jnp.float32, least / len(pieces), top_value / len(pieces)))
        loudness = loudness * jnp.repeat(draws, shape[axis_at] // shards_of).reshape([-1 if axis == axis_at else 1 for axis in range(len(shape))])
    return loudness


def length_profile(amount, total, limit, slope):
    portions = [(1 << 20) // math.isqrt(grade ** slope) + 1 for grade in range(2, amount + 1)]
    rest, holding = total - limit - (amount - 1), [1] * (amount - 1)
    while rest > 0:
        movable = [i for i in range(amount - 1) if holding[i] < limit]
        whole, left = sum([portions[i] for i in movable]), rest
        for i in movable:
            addition = min(limit - holding[i], max(1, left * portions[i] // whole), rest)
            holding[i] = holding[i] + addition
            rest = rest - addition
    return np.array([limit] + holding)


def ragged_sizes(stream_key, number_of, total, bound, skew):
    if number_of == 2:
        one = jax.random.randint(stream_key, (), max(1, total - bound), min(bound, total - 1) + 1)
        return jnp.stack([one, total - one])
    sizes = jnp.asarray(length_profile(number_of, total, bound, skew), jnp.int32)
    pairs = (number_of - 1) // 2
    donor, taker = sizes[1:1 + 2 * pairs:2], sizes[2:2 + 2 * pairs:2]
    room = jnp.minimum(donor - 1, bound - taker)
    moved = jax.random.randint(jax.random.fold_in(stream_key, 1), (pairs,), 0, 1 << 20) % (room + 1)
    sizes = sizes.at[1:1 + 2 * pairs:2].set(donor - moved).at[2:2 + 2 * pairs:2].set(taker + moved)
    return sizes[jax.random.permutation(jax.random.fold_in(stream_key, 2), number_of)]


def bell_draw(stream_key, shape, width, limit, shards=(), kind=jnp.bfloat16):
    factor_of = shard_levels(stream_key, shape, shards, -0.22, 0.18) if shards else 1.0
    entries = jax.random.normal(stream_key, shape, jnp.float32) * width * factor_of
    return jnp.minimum(jnp.maximum(entries, -limit), limit).astype(kind)


def setup_inputs(seed: int = 0) -> dict:
    splits = jax.random.split(jax.random.key(seed), 7)
    q_lin = draw_q_lin(jax.random.fold_in(splits[6], 71), 0)
    k_lin = draw_k_lin(jax.random.fold_in(splits[6], 71), 0)
    v_lin = bell_draw(splits[2], (BATCH, SEQ, HK * HD), 1.0, 6.0, ((0, 32), (1, 16)))
    out_grad = bell_draw(splits[3], (BATCH, SEQ, HQ * HD), 1.0, 6.0, ((0, 32), (1, 16)))
    q_bias = bell_draw(splits[4], (HQ * HD,), 0.5, 3.0, (), jnp.float32)
    doc_lengths = jax.vmap(lambda own: ragged_sizes(own, DOCS, SEQ, LONGEST, 2))(jax.random.split(splits[5], BATCH)).reshape((BATCH, DOCS)).astype(jnp.int32)
    return dict(q_lin=q_lin, k_lin=k_lin, v_lin=v_lin, out_grad=out_grad, q_bias=q_bias, doc_lengths=doc_lengths)


rope_theta = 1000000.0
neg_fill = -1e+30

def rope_tables(positions, head_size):
    half_size = head_size // 2
    exponent = jnp.arange(half_size, dtype=jnp.float32) * (2.0 / head_size)
    inverse_freq = jnp.power(jnp.float32(rope_theta), -exponent)
    angles = positions.astype(jnp.float32)[:, None] * inverse_freq[None, :]
    cosine = jnp.concatenate([jnp.cos(angles), jnp.cos(angles)], axis=1)
    sine_table = jnp.concatenate([jnp.sin(angles), jnp.sin(angles)], axis=1)
    return (cosine, sine_table)

def rotate(vectors, cosine, sine_table, direction):
    half_size = vectors.shape[-1] // 2
    turned = jnp.concatenate([-vectors[..., half_size:], vectors[..., :half_size]], axis=-1)
    return vectors * cosine[:, None, :] + direction * turned * sine_table[:, None, :]

def doc_starts(lengths, positions):
    doc_ends = jnp.cumsum(lengths).astype(jnp.int32)
    before = jnp.where(doc_ends[None, :] <= positions[:, None], lengths[None, :], 0)
    return lax.optimization_barrier(jnp.sum(before, axis=1)).astype(jnp.int32)

def one_sequence(q_lin, k_lin, v_lin, out_grad, lengths, q_bias):
    seq_len = q_lin.shape[0]
    block_rows = seq_len // N_CTX
    kv_heads = k_lin.shape[1] // HD
    q_heads = q_lin.shape[1] // HD
    group_size = q_heads // kv_heads
    score_scale = 1.0 / math.sqrt(HD)
    positions = jnp.arange(seq_len, dtype=jnp.int32)
    starts = doc_starts(lengths, positions)
    cosine, sine_table = rope_tables(positions - starts, HD)
    shifted = (q_lin.astype(jnp.float32) + q_bias).reshape(seq_len, q_heads, HD)
    queries = rotate(shifted, cosine, sine_table, 1.0).astype(jnp.bfloat16)
    rotated_keys = rotate(k_lin.astype(jnp.float32).reshape(seq_len, kv_heads, HD), cosine, sine_table, 1.0).astype(jnp.bfloat16)
    key_floats = rotated_keys.astype(jnp.float32)
    value_floats = v_lin.reshape(seq_len, kv_heads, HD).astype(jnp.float32)
    grad_all = out_grad.reshape(seq_len, kv_heads, group_size, HD)

    def per_block(running, block_index):
        key_acc, value_acc, bias_acc = running
        offset = block_index * block_rows
        q_block = lax.dynamic_slice_in_dim(queries, offset, block_rows, 0).reshape(block_rows, kv_heads, group_size, HD).astype(jnp.float32)
        grad_block = lax.dynamic_slice_in_dim(grad_all, offset, block_rows, 0).astype(jnp.float32)
        row_pos = offset + jnp.arange(block_rows, dtype=jnp.int32)
        row_start = lax.dynamic_slice_in_dim(starts, offset, block_rows, 0)
        cosine_rows = lax.dynamic_slice_in_dim(cosine, offset, block_rows, 0)
        sine_rows = lax.dynamic_slice_in_dim(sine_table, offset, block_rows, 0)
        visible_mask = (positions[None, :] <= row_pos[:, None]) & (positions[None, :] >= row_start[:, None])
        scores = jnp.einsum('rkgd,nkd->kgrn', q_block, key_floats) * score_scale
        row_max = lax.optimization_barrier(jnp.max(jnp.where(visible_mask, scores, neg_fill), axis=-1))
        row_sum = lax.optimization_barrier(jnp.sum(jnp.where(visible_mask, jnp.exp(scores - row_max[..., None]), 0.0), axis=-1))
        log_total = row_max + jnp.log(row_sum)
        weights = jnp.where(visible_mask, jnp.exp(scores - log_total[..., None]), 0.0).astype(jnp.bfloat16)
        weights = lax.optimization_barrier(weights).astype(jnp.float32)
        attended = jnp.einsum('kgrn,nkd->rkgd', weights, value_floats).astype(jnp.bfloat16)
        row_delta = lax.optimization_barrier(jnp.sum(grad_block * attended.astype(jnp.float32), axis=-1)).transpose(1, 2, 0)
        grad_prob = jnp.einsum('rkgd,nkd->kgrn', grad_block, value_floats)
        dscore = (weights * (grad_prob - row_delta[..., None])).astype(jnp.bfloat16)
        dscore = lax.optimization_barrier(dscore).astype(jnp.float32)
        grad_query = score_scale * jnp.einsum('kgrn,nkd->rkgd', dscore, key_floats)
        key_term = (score_scale * jnp.einsum('kgrn,rkgd->nkd', dscore, q_block)).astype(jnp.bfloat16)
        value_term = jnp.einsum('kgrn,rkgd->nkd', weights, grad_block).astype(jnp.bfloat16)
        grad_pre = rotate(grad_query.reshape(block_rows, q_heads, HD), cosine_rows, sine_rows, -1.0)
        key_acc = key_acc + key_term.astype(jnp.float32)
        value_acc = value_acc + value_term.astype(jnp.float32)
        bias_acc = bias_acc + lax.optimization_barrier(jnp.sum(grad_pre, axis=0)).reshape(-1)
        outputs = (attended.reshape(block_rows, q_heads * HD), grad_pre.reshape(block_rows, q_heads * HD).astype(jnp.bfloat16))
        return ((key_acc, value_acc, bias_acc), outputs)
    zero_kv = jnp.zeros((seq_len, kv_heads, HD), jnp.float32)
    zero_bias = jnp.zeros((q_heads * HD,), jnp.float32)
    final, stacked = lax.scan(per_block, (zero_kv, zero_kv, zero_bias), jnp.arange(N_CTX, dtype=jnp.int32))
    key_acc, value_acc, bias_acc = final
    attended = stacked[0].reshape(seq_len, q_heads * HD)
    grad_q = stacked[1].reshape(seq_len, q_heads * HD)
    grad_k = rotate(key_acc, cosine, sine_table, -1.0).astype(jnp.bfloat16).reshape(seq_len, kv_heads * HD)
    grad_v = value_acc.astype(jnp.bfloat16).reshape(seq_len, kv_heads * HD)
    return (attended, grad_q, grad_k, grad_v, bias_acc)

def reference(q_lin, k_lin, v_lin, out_grad, q_bias, doc_lengths):

    def per_sequence(inputs):
        return one_sequence(inputs[0], inputs[1], inputs[2], inputs[3], inputs[4], q_bias)
    attended, grad_q, grad_k, grad_v, bias_parts = lax.map(per_sequence, (q_lin, k_lin, v_lin, out_grad, doc_lengths))
    token_total = q_lin.shape[0] * q_lin.shape[1]
    bias_grad = lax.optimization_barrier(jnp.sum(bias_parts, axis=0)) / jnp.float32(math.sqrt(token_total))
    return (attended, grad_q, grad_k, grad_v, bias_grad)
```

```python
import math

import jax
import jax.numpy as jnp
import numpy as np
from jax import lax
from jax.experimental import pallas as pl
from jax.experimental.pallas import tpu as pltpu
from jax.sharding import PartitionSpec as P

HD = 128
ROWS = 128
SIDE = 4
WINDOW = 10
SLOTS = 13
PAIRS = WINDOW // 2
THETA = 1000000.0
FILL = -1e30
MESH = pl.DeviceIdType.MESH
F32 = jnp.float32
BF16 = jnp.bfloat16


def dp_stages(size):
    if size == 32:
        return [(1, 2), (2, 4), (8, 4)]
    return [(1, size)] if size > 1 else []


def need(dr, reader, col):
    if dr == 0:
        return col < reader
    if dr == 1:
        return col >= 0
    return col >= reader - 1


def kernel(
    dp_size, group, q_ref, k_ref, v_ref, do_ref, bias_ref, len_ref, freq_ref,
    att_ref, gq_ref, gk_ref, gv_ref, bg_ref,
    kbuf, vbuf, qs, dos, s_ref, w_ref, mx_ref, acc_ref, stat_ref,
    gkb, gvb, far_k, far_v, nl_k, nl_v, nr_k, nr_v, rz_k, rz_v, zs_k, zs_v, sp_k, sp_v,
    acck, accv, bst, cos_ref, sin_ref, start_ref,
    send_sems, krecv, vrecv, rrecv, brecv,
):
    c = lax.axis_index("ctx")
    d = lax.axis_index("dp")
    x = lax.rem(c, SIDE)
    z = lax.div(c, SIDE)
    base = z * SIDE
    xr, xl, xo = lax.rem(x + 1, SIDE), lax.rem(x + 3, SIDE), lax.rem(x + 2, SIDE)
    right, left = base + xr, base + xl
    scale = 1.0 / math.sqrt(HD)
    heads = 2 * group
    special_from, special_to = c == 3, c == 12

    barrier = pltpu.get_barrier_semaphore()
    stages = [("ctx", 1, SIDE), ("ctx", SIDE, SIDE)]
    stages += [("dp", stride, size) for stride, size in dp_stages(dp_size)]

    def peer(axis, stride, size, step):
        me = c if axis == "ctx" else d
        at = lax.rem(lax.div(me, stride), size)
        other = lax.rem(at + step, size)
        return me + (other - at) * stride, at, other

    count = 0
    for axis, stride, size in stages:
        for step in range(1, size):
            target, _, _ = peer(axis, stride, size, step)
            pl.semaphore_signal(barrier, inc=1, device_id={axis: target}, device_id_type=MESH)
            count += 1

    @pl.when(special_from)
    def _():
        pl.semaphore_signal(barrier, inc=1, device_id={"ctx": c + 9}, device_id_type=MESH)

    @pl.when(special_to)
    def _():
        pl.semaphore_signal(barrier, inc=1, device_id={"ctx": c - 9}, device_id_type=MESH)

    pl.semaphore_wait(barrier, count + jnp.where(special_from | special_to, 1, 0))

    pending = []

    def slot(buf, s, blocks=1):
        return buf.at[pl.ds(pl.multiple_of(s * ROWS, ROWS), blocks * ROWS)]

    def send(pred, src, dst, recv_sem, target, axis="ctx"):
        copy = pltpu.make_async_remote_copy(
            src_ref=src, dst_ref=dst, send_sem=send_sems.at[len(pending)], recv_sem=recv_sem,
            device_id={axis: target}, device_id_type=MESH,
        )
        pending.append((pred, copy))

        @pl.when(pred)
        def _():
            copy.start()

    def arrived(pred, dst, recv_sem):
        copy = pltpu.make_async_remote_copy(
            src_ref=dst, dst_ref=dst, send_sem=send_sems.at[0], recv_sem=recv_sem,
            device_id={"ctx": right}, device_id_type=MESH,
        )

        @pl.when(pred)
        def _():
            copy.wait_recv()

    def first(dr):
        return 9 - SIDE * dr

    def own_send(buf, recv, is_key):
        own = slot(buf, 9 + x)
        sem = recv.at[9 + x]
        far = need(0, xo, x)
        to_right, to_left = need(0, xr, x), need(0, xl, x)
        send(z < 3, own, slot(buf, 5 + x), recv.at[5 + x], c + 4)
        send(z < 2, own, slot(buf, 1 + x), recv.at[1 + x], c + 8)
        send(to_right | far if is_key else to_right, own, own, sem, right)
        send(to_left if is_key else to_left | far, own, own, sem, left)
        send(special_from, own, slot(buf, 0), recv.at[0], c + 9)

    def relay(buf, recv, is_key, dr):
        valid = z >= dr
        s = first(dr) + x
        own, sem = slot(buf, s), recv.at[s]
        arrived(valid, own, sem)
        far = need(dr, xo, x)
        to_right, to_left = need(dr, xr, x), need(dr, xl, x)
        send(valid & (to_right | far if is_key else to_right), own, own, sem, right)
        send(valid & (to_left if is_key else to_left | far), own, own, sem, left)

    def forward(dr):
        valid = z >= dr
        sl, sr = first(dr) + xl, first(dr) + xr
        kl, kr, vl, vr = slot(kbuf, sl), slot(kbuf, sr), slot(vbuf, sl), slot(vbuf, sr)
        arrived(valid & (need(dr, x, xl) | need(dr, xr, xl)), kl, krecv.at[sl])
        send(valid & need(dr, xr, xl), kl, kl, krecv.at[sl], right)
        arrived(valid & (need(dr, x, xr) | need(dr, xl, xr)), vr, vrecv.at[sr])
        send(valid & need(dr, xl, xr), vr, vr, vrecv.at[sr], left)
        arrived(valid & need(dr, x, xr), kr, krecv.at[sr])
        arrived(valid & need(dr, x, xl), vl, vrecv.at[sl])

    def last(dr):
        valid = z >= dr
        so = first(dr) + xo
        arrived(valid & need(dr, x, xo), slot(kbuf, so), krecv.at[so])
        arrived(valid & need(dr, x, xo), slot(vbuf, so), vrecv.at[so])

    vbuf[pl.ds(pl.multiple_of((9 + x) * ROWS, ROWS), ROWS), :] = v_ref[...]
    own_send(vbuf, vrecv, False)

    pos = c * ROWS + lax.broadcasted_iota(jnp.int32, (ROWS, HD), 0)
    start = jnp.zeros((ROWS, HD), jnp.int32)
    end = jnp.int32(0)
    for i in range(len_ref.shape[1]):
        length = len_ref[0, i]
        end = end + length
        start = start + jnp.where(end <= pos, length, 0)
    start_ref[...] = start
    angle = (pos - start).astype(F32) * freq_ref[...]
    lane = lax.broadcasted_iota(jnp.int32, (ROWS, HD), 1)
    cos_ref[...] = jnp.cos(angle)
    sine = jnp.sin(angle)
    sin_ref[...] = jnp.where(lane < HD // 2, -sine, sine)

    def rope(value):
        return value * cos_ref[...] + pltpu.roll(value, HD // 2, 1) * sin_ref[...]

    def rope_back(value):
        return value * cos_ref[...] - pltpu.roll(value, HD // 2, 1) * sin_ref[...]

    own_rows = pl.ds(pl.multiple_of((9 + x) * ROWS, ROWS), ROWS)
    for g in range(2):
        cols = slice(g * HD, (g + 1) * HD)
        kbuf[own_rows, cols] = rope(k_ref[:, cols].astype(F32)).astype(BF16)
    own_send(kbuf, krecv, True)

    def clear(s):
        rows = pl.ds(pl.multiple_of(s * ROWS, ROWS), ROWS)
        kbuf[rows, :] = jnp.zeros((ROWS, 2 * HD), BF16)
        vbuf[rows, :] = jnp.zeros((ROWS, 2 * HD), BF16)

    for dr in (1, 2):

        @pl.when(z < dr)
        def _():
            for i in range(SIDE):
                clear(jnp.int32(first(dr) + i))

    @pl.when(c != 12)
    def _():
        clear(jnp.int32(0))

    @pl.when(x == 0)
    def _():
        gvb[10 * ROWS : 11 * ROWS, :] = jnp.zeros((ROWS, 2 * HD), BF16)

    for h in range(heads):
        g, r = h // group, (h % group) * ROWS
        cols = slice(h * HD, (h + 1) * HD)
        qs[g, r : r + ROWS, :] = rope(q_ref[:, cols].astype(F32) + bias_ref[:, cols]).astype(BF16)
        dos[g, r : r + ROWS, :] = do_ref[:, cols]

    for dr in (1, 2):
        relay(vbuf, vrecv, False, dr)
        relay(kbuf, krecv, True, dr)
    for dr in (0, 1, 2):
        forward(dr)
    for dr in (0, 1, 2):
        last(dr)
    arrived(special_to, slot(kbuf, 0), krecv.at[0])
    arrived(special_to, slot(vbuf, 0), vrecv.at[0])

    nt = (((1,), (1,)), ((), ()))
    tn = (((0,), (0,)), ((), ()))
    nn = (((1,), (0,)), ((), ()))

    def window(p):
        return pl.ds(pl.multiple_of((x + 2 * p) * ROWS, ROWS), 2 * ROWS)

    first_key = (c - (WINDOW - 1)) * ROWS

    for g in range(2):
        mx_ref[g] = jnp.full((group * ROWS, HD), FILL, F32)

    def score_step(p, carry):
        key_pos = first_key + p * 2 * ROWS + lax.broadcasted_iota(jnp.int32, (ROWS, 2 * ROWS), 1)
        row = c * ROWS + lax.broadcasted_iota(jnp.int32, (ROWS, 2 * ROWS), 0)
        begin = jnp.concatenate([start_ref[...], start_ref[...]], axis=1)
        visible = (key_pos <= row) & (key_pos >= begin)
        for g in range(2):
            keys = kbuf[window(p), g * HD : (g + 1) * HD]
            raw = lax.dot_general(qs[g], keys, nt, preferred_element_type=F32)
            for h in range(group):
                rows = slice(h * ROWS, (h + 1) * ROWS)
                part = jnp.where(visible, raw[rows], FILL)
                s_ref[g, p, rows] = part
                mx_ref[g, rows] = jnp.maximum(
                    mx_ref[g, rows], jnp.maximum(part[:, :HD], part[:, HD:])
                )
        return carry

    lax.fori_loop(0, PAIRS, score_step, 0)

    factor = scale * math.log2(math.e)

    for g in range(2):
        for h in range(group):
            rows = slice(h * ROWS, (h + 1) * ROWS)
            top = jnp.max(mx_ref[g, rows], axis=1, keepdims=True)
            mx_ref[g, rows] = jnp.broadcast_to(top, (ROWS, HD))
        acc_ref[g] = jnp.zeros((group * ROWS, HD), F32)

    def exp_step(p, carry):
        for g in range(2):
            for h in range(group):
                rows = slice(h * ROWS, (h + 1) * ROWS)
                top = mx_ref[g, rows]
                lo = jnp.exp2((s_ref[g, p, rows, :HD] - top) * factor)
                hi = jnp.exp2((s_ref[g, p, rows, HD:] - top) * factor)
                s_ref[g, p, rows, :HD] = lo
                s_ref[g, p, rows, HD:] = hi
                acc_ref[g, rows] += lo + hi
        return carry

    lax.fori_loop(0, PAIRS, exp_step, 0)

    for g in range(2):
        for h in range(group):
            rows = slice(h * ROWS, (h + 1) * ROWS)
            total = jnp.sum(acc_ref[g, rows], axis=1, keepdims=True)
            stat_ref[g, rows] = jnp.broadcast_to(1.0 / total, (ROWS, HD))
        acc_ref[g] = jnp.zeros((group * ROWS, HD), F32)

    def out_step(p, carry):
        for g in range(2):
            inverse = stat_ref[g]
            lo = (s_ref[g, p, :, :HD] * inverse).astype(BF16)
            hi = (s_ref[g, p, :, HD:] * inverse).astype(BF16)
            weights = jnp.concatenate([lo, hi], axis=1)
            w_ref[g, p] = weights
            values = vbuf[window(p), g * HD : (g + 1) * HD]
            acc_ref[g] += lax.dot_general(weights, values, nn, preferred_element_type=F32)
        return carry

    lax.fori_loop(0, PAIRS, out_step, 0)

    for g in range(2):
        for h in range(group):
            rows = slice(h * ROWS, (h + 1) * ROWS)
            attended = acc_ref[g, rows].astype(BF16)
            at = (g * group + h) * HD
            att_ref[:, at : at + HD] = attended
            delta = jnp.sum(
                dos[g, rows].astype(F32) * attended.astype(F32), axis=1, keepdims=True
            )
            stat_ref[g, rows] = jnp.broadcast_to(delta, (ROWS, HD))
        acc_ref[g] = jnp.zeros((group * ROWS, HD), F32)

    def grad_step(p, carry):
        for g in range(2):
            cols = slice(g * HD, (g + 1) * HD)
            keys, values = kbuf[window(p), cols], vbuf[window(p), cols]
            prob = lax.dot_general(dos[g], values, nt, preferred_element_type=F32)
            delta = stat_ref[g]
            weights = w_ref[g, p]
            lo = weights[:, :HD].astype(F32) * (prob[:, :HD] - delta)
            hi = weights[:, HD:].astype(F32) * (prob[:, HD:] - delta)
            dscore = jnp.concatenate([lo.astype(BF16), hi.astype(BF16)], axis=1)
            acc_ref[g] += lax.dot_general(dscore, keys, nn, preferred_element_type=F32)
            key_term = lax.dot_general(dscore, qs[g], tn, preferred_element_type=F32)
            value_term = lax.dot_general(weights, dos[g], tn, preferred_element_type=F32)
            gkb[window(p), cols] = (scale * key_term).astype(BF16)
            gvb[window(p), cols] = value_term.astype(BF16)
        return carry

    def back_far(dr):
        so = first(dr) + xo
        pred = (z >= dr) & need(dr, x, xo)
        send(pred, slot(gkb, so), far_k.at[dr], rrecv.at[dr, 0], left)
        send(pred, slot(gvb, so), far_v.at[dr], rrecv.at[dr, 1], right)

    def add_into(buf, s, other):
        rows = pl.ds(pl.multiple_of(s * ROWS, ROWS), ROWS)
        buf[rows, :] = (buf[rows, :].astype(F32) + other[...].astype(F32)).astype(BF16)

    def back_near(dr):
        valid = z >= dr
        sl, sr = first(dr) + xl, first(dr) + xr
        send(valid & need(dr, x, xl), slot(gvb, sl), nr_v.at[dr], rrecv.at[dr, 3], left)
        send(valid & need(dr, x, xr), slot(gkb, sr), nl_k.at[dr], rrecv.at[dr, 4], right)
        got = valid & need(dr, xr, xl)
        arrived(got, far_k.at[dr], rrecv.at[dr, 0])

        @pl.when(got)
        def _():
            add_into(gkb, sl, far_k.at[dr])

        pred = valid & (need(dr, x, xl) | need(dr, xr, xl))
        send(pred, slot(gkb, sl), nr_k.at[dr], rrecv.at[dr, 2], left)
        got_v = valid & need(dr, xl, xr)
        arrived(got_v, far_v.at[dr], rrecv.at[dr, 1])

        @pl.when(got_v)
        def _():
            add_into(gvb, sr, far_v.at[dr])

        pred = valid & (need(dr, x, xr) | need(dr, xl, xr))
        send(pred, slot(gvb, sr), nl_v.at[dr], rrecv.at[dr, 5], right)

    def add_when(pred, acc, src, sem):
        arrived(pred, src, sem)

        @pl.when(pred)
        def _():
            acc[...] += src[...].astype(F32)

    def back_sum(dr):
        valid = z >= dr
        so = pl.ds(pl.multiple_of((first(dr) + x) * ROWS, ROWS), ROWS)
        acck[...] = gkb[so, :].astype(F32)
        accv[...] = gvb[so, :].astype(F32)
        near_l, near_r, far = need(dr, xl, x), need(dr, xr, x), need(dr, xo, x)
        add_when(valid & near_r, accv, nr_v.at[dr], rrecv.at[dr, 3])
        add_when(valid & near_l, acck, nl_k.at[dr], rrecv.at[dr, 4])
        add_when(valid & (near_r | far), acck, nr_k.at[dr], rrecv.at[dr, 2])
        add_when(valid & (near_l | far), accv, nl_v.at[dr], rrecv.at[dr, 5])
        if dr:
            zs_k[dr - 1] = acck[...].astype(BF16)
            zs_v[dr - 1] = accv[...].astype(BF16)
            down = c - SIDE * dr
            send(valid, zs_k.at[dr - 1], rz_k.at[dr - 1], rrecv.at[dr, 6], down)
            send(valid, zs_v.at[dr - 1], rz_v.at[dr - 1], rrecv.at[dr, 7], down)

    lax.fori_loop(0, 3, grad_step, 0)
    back_far(2)
    send(special_to, slot(gkb, 0), sp_k, rrecv.at[0, 6], c - 9)
    send(special_to, slot(gvb, 0), sp_v, rrecv.at[0, 7], c - 9)
    back_near(2)
    lax.fori_loop(3, PAIRS, grad_step, 0)
    back_far(1)
    back_far(0)
    back_near(1)
    back_near(0)
    back_sum(2)

    for h in range(heads):
        g, r = h // group, (h % group) * ROWS
        cols = slice(h * HD, (h + 1) * HD)
        before = rope_back(scale * acc_ref[g, r : r + ROWS])
        gq_ref[:, cols] = before.astype(BF16)
        bst[0, x, h : h + 1, :] = jnp.sum(before, axis=0, keepdims=True)
    pad = bst.shape[2] - heads
    if pad:
        bst[0, x, heads:, :] = jnp.zeros((pad, HD), F32)

    def bias_start(i):
        axis, stride, size = stages[i]
        for step in range(1, size):
            target, at, _ = peer(axis, stride, size, step)
            send(c >= 0, bst.at[i, at], bst.at[i, at], brecv.at[i, at], target, axis)

    def bias_end(i):
        axis, stride, size = stages[i]
        for step in range(1, size):
            _, _, other = peer(axis, stride, size, step)
            arrived(c >= 0, bst.at[i, other], brecv.at[i, other])
        total = bst[i, 0]
        for j in range(1, size):
            total = total + bst[i, j]
        if i + 1 < len(stages):
            axis, stride, size = stages[i + 1]
            _, at, _ = peer(axis, stride, size, 1)
            bst[i + 1, at] = total
            bias_start(i + 1)
        else:
            total = total * (1.0 / math.sqrt(dp_size * SIDE * SIDE * ROWS))
            for h in range(heads):
                bg_ref[:, h * HD : (h + 1) * HD] = total[h : h + 1]

    bias_start(0)
    back_sum(1)
    bias_end(0)
    back_sum(0)
    bias_end(1)
    for dr in (2, 1):
        add_when(z + dr < SIDE, acck, rz_k.at[dr - 1], rrecv.at[dr, 6])
        add_when(z + dr < SIDE, accv, rz_v.at[dr - 1], rrecv.at[dr, 7])
    add_when(special_from, acck, sp_k, rrecv.at[0, 6])
    add_when(special_from, accv, sp_v, rrecv.at[0, 7])
    for g in range(2):
        cols = slice(g * HD, (g + 1) * HD)
        gk_ref[:, cols] = rope_back(acck[:, cols]).astype(BF16)
    gv_ref[...] = accv[...].astype(BF16)
    for i in range(2, len(stages)):
        bias_end(i)

    for pred, copy in pending:

        @pl.when(pred)
        def _():
            copy.wait_send()


def shards(q_lin, k_lin, v_lin, out_grad, q_bias, doc_lengths):
    width = q_lin.shape[2]
    heads = width // HD
    group = heads // 2
    dp_size = lax.axis_size("dp")
    exponent = np.arange(HD // 2, dtype=np.float32) * np.float32(2.0 / HD)
    freq = np.power(np.float32(THETA), -exponent).astype(np.float32)
    freq = jnp.asarray(np.concatenate([freq, freq])[None, :])
    rows = group * ROWS
    vmem = pl.BlockSpec(memory_space=pltpu.VMEM)
    block = lambda *lead: pltpu.VMEM((*lead, ROWS, 2 * HD), BF16)
    n_stage = 2 + len(dp_stages(dp_size))
    pad_heads = -(-heads // 8) * 8
    outs = pl.pallas_call(
        lambda *refs: kernel(dp_size, group, *refs),
        out_shape=(
            jax.ShapeDtypeStruct((ROWS, width), BF16),
            jax.ShapeDtypeStruct((ROWS, width), BF16),
            jax.ShapeDtypeStruct((ROWS, 2 * HD), BF16),
            jax.ShapeDtypeStruct((ROWS, 2 * HD), BF16),
            jax.ShapeDtypeStruct((1, width), F32),
        ),
        in_specs=[vmem] * 5 + [pl.BlockSpec(memory_space=pltpu.SMEM), vmem],
        out_specs=(vmem,) * 5,
        scratch_shapes=[
            pltpu.VMEM((SLOTS * ROWS, 2 * HD), BF16),
            pltpu.VMEM((SLOTS * ROWS, 2 * HD), BF16),
            pltpu.VMEM((2, rows, HD), BF16),
            pltpu.VMEM((2, rows, HD), BF16),
            pltpu.VMEM((2, PAIRS, rows, 2 * ROWS), F32),
            pltpu.VMEM((2, PAIRS, rows, 2 * ROWS), BF16),
            pltpu.VMEM((2, rows, HD), F32),
            pltpu.VMEM((2, rows, HD), F32),
            pltpu.VMEM((2, rows, HD), F32),
            pltpu.VMEM((SLOTS * ROWS, 2 * HD), BF16),
            pltpu.VMEM((SLOTS * ROWS, 2 * HD), BF16),
            block(3), block(3), block(3), block(3), block(3), block(3),
            block(2), block(2), block(2), block(2), block(), block(),
            pltpu.VMEM((ROWS, 2 * HD), F32),
            pltpu.VMEM((ROWS, 2 * HD), F32),
            pltpu.VMEM((n_stage, SIDE, pad_heads, HD), F32),
            pltpu.VMEM((ROWS, HD), F32),
            pltpu.VMEM((ROWS, HD), F32),
            pltpu.VMEM((ROWS, HD), jnp.int32),
            pltpu.SemaphoreType.DMA((72,)),
            pltpu.SemaphoreType.DMA((SLOTS,)),
            pltpu.SemaphoreType.DMA((SLOTS,)),
            pltpu.SemaphoreType.DMA((3, 8)),
            pltpu.SemaphoreType.DMA((n_stage, SIDE)),
        ],
        compiler_params=pltpu.CompilerParams(
            collective_id=0, has_side_effects=True, vmem_limit_bytes=56 * 1024 * 1024
        ),
        cost_estimate=pl.CostEstimate(
            flops=12 * heads * ROWS * WINDOW * ROWS * HD,
            bytes_accessed=4 * 2 * ROWS * width,
            transcendentals=heads * ROWS * WINDOW * ROWS,
        ),
    )(
        q_lin.reshape(ROWS, width), k_lin.reshape(ROWS, 2 * HD), v_lin.reshape(ROWS, 2 * HD),
        out_grad.reshape(ROWS, width), q_bias.reshape(1, width), doc_lengths, freq,
    )
    attended, grad_q, grad_k, grad_v, bias_grad = outs
    return (attended[None], grad_q[None], grad_k[None], grad_v[None], bias_grad.reshape(width))


def solution(mesh):
    rows = P("dp", "ctx", None)
    return jax.shard_map(
        shards,
        mesh=mesh,
        in_specs=(rows, rows, rows, rows, P(), P("dp", None)),
        out_specs=(rows, rows, rows, rows, P()),
        check_vma=False,
    )
```

```python
import math

import jax
import jax.numpy as jnp
import numpy as np
from jax import lax
from jax.experimental import pallas as pl
from jax.experimental.pallas import tpu as pltpu
from jax.sharding import PartitionSpec as P

HD = 128
ROWS = 128
SIDE = 4
WINDOW = 10
SLOTS = 13
PAIRS = WINDOW // 2
THETA = 1000000.0
FILL = -1e30
MESH = pl.DeviceIdType.MESH
F32 = jnp.float32
BF16 = jnp.bfloat16


def bias_stages(dp_size):
    if dp_size == 32:
        return [("z", 4 * SIDE), ("x", SIDE), ("yc", 2 * SIDE)]
    return [("z", SIDE), ("x", SIDE)]


def need(dr, reader, col):
    if dr == 0:
        return col < reader
    if dr == 1:
        return col >= 0
    return col >= reader - 1


def kernel(
    dp_size, group, q_hbm, k_hbm, v_hbm, do_hbm, bias_ref, len_ref, freq_ref,
    att_hbm, gq_hbm, gk_hbm, gv_hbm, bg_ref,
    q_ref, k_ref, v_ref, do_ref, att_ref, gq_ref, gk_ref, gv_ref,
    kbuf, vbuf, qs, dos, s_ref, p_ref, w_ref, ds_ref, mx_ref, acc_ref, stat_ref,
    gkb, gvb, far_k, far_v, nl_k, nl_v, nr_k, nr_v, rz_k, rz_v, zs_k, zs_v, sp_k, sp_v,
    acck, accv, bst, cos_ref, sin_ref, start_ref,
    send_sems, krecv, vrecv, rrecv, brecv, local_sems,
):
    c = lax.axis_index("ctx")
    d = lax.axis_index("dp")
    x = lax.rem(c, SIDE)
    z = lax.div(c, SIDE)
    base = z * SIDE
    xr, xl, xo = lax.rem(x + 1, SIDE), lax.rem(x + 3, SIDE), lax.rem(x + 2, SIDE)
    right, left = base + xr, base + xl
    scale = 1.0 / math.sqrt(HD)
    heads = 2 * group
    special_from, special_to = c == 3, c == 12

    def load(src, dst, i):
        pltpu.make_async_copy(src, dst, local_sems.at[i]).start()

    def loaded(src, dst, i):
        pltpu.make_async_copy(src, dst, local_sems.at[i]).wait()

    barrier = pltpu.get_barrier_semaphore()
    stages = bias_stages(dp_size)

    def peer(kind, size, step):
        if kind == "x":
            other = lax.rem(x + step, SIDE)
            return {"ctx": base + other}, x, other
        if kind == "z":
            high = lax.rem(lax.div(d, 2), SIDE) if size > SIDE else 0
            at = high * SIDE + z
            other = lax.rem(at + step, size)
            ctx = lax.rem(other, SIDE) * SIDE + x
            return {"dp": d + (lax.div(other, SIDE) - high) * 2, "ctx": ctx}, at, other
        y, core = lax.div(d, 8), lax.rem(d, 2)
        at = y * 2 + core
        other = lax.rem(at + step, size)
        move = (lax.div(other, 2) - y) * 8 + lax.rem(other, 2) - core
        return {"dp": d + move}, at, other

    count = jnp.where(special_from | special_to, 1, 0)
    for kind, size in stages:
        for step in range(1, size):
            target, _, _ = peer(kind, size, step)
            pl.semaphore_signal(barrier, inc=1, device_id=target, device_id_type=MESH)
        count = count + (size - 1)

    @pl.when(special_from)
    def _():
        pl.semaphore_signal(barrier, inc=1, device_id={"ctx": c + 9}, device_id_type=MESH)

    @pl.when(special_to)
    def _():
        pl.semaphore_signal(barrier, inc=1, device_id={"ctx": c - 9}, device_id_type=MESH)

    load(q_hbm, q_ref, 0)
    load(do_hbm, do_ref, 1)
    load(k_hbm, k_ref, 2)
    load(v_hbm, v_ref, 3)
    pl.semaphore_wait(barrier, count)

    pending = []

    def slot(buf, s, blocks=1):
        return buf.at[pl.ds(pl.multiple_of(s * ROWS, ROWS), blocks * ROWS)]

    def send(pred, src, dst, recv_sem, target):
        target = target if isinstance(target, dict) else {"ctx": target}
        copy = pltpu.make_async_remote_copy(
            src_ref=src, dst_ref=dst, send_sem=send_sems.at[len(pending)], recv_sem=recv_sem,
            device_id=target, device_id_type=MESH,
        )
        pending.append((pred, copy))

        @pl.when(pred)
        def _():
            copy.start()

    def arrived(pred, dst, recv_sem):
        copy = pltpu.make_async_remote_copy(
            src_ref=dst, dst_ref=dst, send_sem=send_sems.at[0], recv_sem=recv_sem,
            device_id={"ctx": right}, device_id_type=MESH,
        )

        @pl.when(pred)
        def _():
            copy.wait_recv()

    def first(dr):
        return 9 - SIDE * dr

    def far_path(dr):
        return dr != 2

    def spread(buf, recv, is_key, dr):
        valid = z >= dr
        s = first(dr) + x
        own, sem = slot(buf, s), recv.at[s]
        if dr:
            arrived(valid, own, sem)
        if dr < 2:
            up = slot(buf, s - SIDE)
            send(valid & (z < SIDE - 1), own, up, recv.at[s - SIDE], c + SIDE)
        far = need(dr, xo, x)
        if not far_path(dr):
            send(valid & far, own, own, sem, base + xo)
        to_right, to_left = need(dr, xr, x), need(dr, xl, x)
        on_right, on_left = far_path(dr) & is_key, far_path(dr) & (not is_key)
        send(valid & (to_right | far if on_right else to_right), own, own, sem, right)
        send(valid & (to_left | far if on_left else to_left), own, own, sem, left)
        if dr == 0:
            send(special_from, own, slot(buf, 0), recv.at[0], c + 9)

    def forward(dr):
        valid = z >= dr
        sl, sr = first(dr) + xl, first(dr) + xr
        kl, kr, vl, vr = slot(kbuf, sl), slot(kbuf, sr), slot(vbuf, sl), slot(vbuf, sr)
        use_l, use_r = need(dr, x, xl), need(dr, x, xr)
        if far_path(dr):
            on_v, on_k = need(dr, xl, xr), need(dr, xr, xl)
            arrived(valid & (use_r | on_v), vr, vrecv.at[sr])
            send(valid & on_v, vr, vr, vrecv.at[sr], left)
            arrived(valid & (use_l | on_k), kl, krecv.at[sl])
            send(valid & on_k, kl, kl, krecv.at[sl], right)
        else:
            arrived(valid & use_r, vr, vrecv.at[sr])
            arrived(valid & use_l, kl, krecv.at[sl])
        arrived(valid & use_l, vl, vrecv.at[sl])
        arrived(valid & use_r, kr, krecv.at[sr])

    def last(dr):
        valid = z >= dr
        so = first(dr) + xo
        arrived(valid & need(dr, x, xo), slot(kbuf, so), krecv.at[so])
        arrived(valid & need(dr, x, xo), slot(vbuf, so), vrecv.at[so])

    loaded(v_hbm, v_ref, 3)
    vbuf[pl.ds(pl.multiple_of((9 + x) * ROWS, ROWS), ROWS), :] = v_ref[...]
    spread(vbuf, vrecv, False, 0)

    pos = c * ROWS + lax.broadcasted_iota(jnp.int32, (ROWS, HD), 0)
    start = jnp.zeros((ROWS, HD), jnp.int32)
    end = jnp.int32(0)
    for i in range(len_ref.shape[1]):
        length = len_ref[0, i]
        end = end + length
        start = start + jnp.where(end <= pos, length, 0)
    start_ref[...] = start
    angle = (pos - start).astype(F32) * freq_ref[...]
    lane = lax.broadcasted_iota(jnp.int32, (ROWS, HD), 1)
    cos_ref[...] = jnp.cos(angle)
    sine = jnp.sin(angle)
    sin_ref[...] = jnp.where(lane < HD // 2, -sine, sine)

    def rope(value):
        return value * cos_ref[...] + pltpu.roll(value, HD // 2, 1) * sin_ref[...]

    def rope_back(value):
        return value * cos_ref[...] - pltpu.roll(value, HD // 2, 1) * sin_ref[...]

    loaded(k_hbm, k_ref, 2)
    own_rows = pl.ds(pl.multiple_of((9 + x) * ROWS, ROWS), ROWS)
    for g in range(2):
        cols = slice(g * HD, (g + 1) * HD)
        kbuf[own_rows, cols] = rope(k_ref[:, cols].astype(F32)).astype(BF16)
    spread(kbuf, krecv, True, 0)

    def clear(s):
        rows = pl.ds(pl.multiple_of(s * ROWS, ROWS), ROWS)
        kbuf[rows, :] = jnp.zeros((ROWS, 2 * HD), BF16)
        vbuf[rows, :] = jnp.zeros((ROWS, 2 * HD), BF16)

    for dr in (1, 2):

        @pl.when(z < dr)
        def _():
            for i in range(SIDE):
                clear(jnp.int32(first(dr) + i))

    @pl.when(c != 12)
    def _():
        clear(jnp.int32(0))

    @pl.when(x == 0)
    def _():
        gvb[10 * ROWS : 11 * ROWS, :] = jnp.zeros((ROWS, 2 * HD), BF16)

    loaded(q_hbm, q_ref, 0)
    loaded(do_hbm, do_ref, 1)
    for h in range(heads):
        g, r = h // group, (h % group) * ROWS
        cols = slice(h * HD, (h + 1) * HD)
        qs[g, r : r + ROWS, :] = rope(q_ref[:, cols].astype(F32) + bias_ref[cols]).astype(BF16)
        dos[g, r : r + ROWS, :] = do_ref[:, cols]

    nt = (((1,), (1,)), ((), ()))
    tn = (((0,), (0,)), ((), ()))
    nn = (((1,), (0,)), ((), ()))

    def window(p):
        return pl.ds(pl.multiple_of((x + 2 * p) * ROWS, ROWS), 2 * ROWS)

    first_key = (c - (WINDOW - 1)) * ROWS

    for g in range(2):
        mx_ref[g] = jnp.full((group * ROWS, HD), FILL, F32)

    def score_step(p):
        key_pos = first_key + p * 2 * ROWS + lax.broadcasted_iota(jnp.int32, (ROWS, 2 * ROWS), 1)
        row = c * ROWS + lax.broadcasted_iota(jnp.int32, (ROWS, 2 * ROWS), 0)
        begin = jnp.concatenate([start_ref[...], start_ref[...]], axis=1)
        visible = (key_pos <= row) & (key_pos >= begin)
        for g in range(2):
            keys = kbuf[window(p), g * HD : (g + 1) * HD]
            raw = lax.dot_general(qs[g], keys, nt, preferred_element_type=F32)
            for h in range(group):
                rows = slice(h * ROWS, (h + 1) * ROWS)
                part = jnp.where(visible, raw[rows], FILL)
                s_ref[g, p, rows] = part
                mx_ref[g, rows] = jnp.maximum(
                    mx_ref[g, rows], jnp.maximum(part[:, :HD], part[:, HD:])
                )
            values = vbuf[window(p), g * HD : (g + 1) * HD]
            p_ref[g, p] = lax.dot_general(dos[g], values, nt, preferred_element_type=F32)
        return 0

    spread(vbuf, vrecv, False, 1)
    spread(kbuf, krecv, True, 1)
    forward(0)
    spread(vbuf, vrecv, False, 2)
    spread(kbuf, krecv, True, 2)
    forward(1)
    score_step(4)
    forward(2)
    arrived(special_to, slot(kbuf, 0), krecv.at[0])
    arrived(special_to, slot(vbuf, 0), vrecv.at[0])
    lax.fori_loop(0, 2, lambda i, carry: score_step(2 - 2 * i), 0)
    last(0)
    last(1)
    last(2)
    lax.fori_loop(0, 2, lambda i, carry: score_step(3 - 2 * i), 0)

    factor = scale * math.log2(math.e)

    for g in range(2):
        for h in range(group):
            rows = slice(h * ROWS, (h + 1) * ROWS)
            top = jnp.max(mx_ref[g, rows], axis=1, keepdims=True)
            mx_ref[g, rows] = jnp.broadcast_to(top, (ROWS, HD))
        acc_ref[g] = jnp.zeros((group * ROWS, HD), F32)

    def exp_step(p, carry):
        for g in range(2):
            for h in range(group):
                rows = slice(h * ROWS, (h + 1) * ROWS)
                top = mx_ref[g, rows]
                lo = jnp.exp2((s_ref[g, p, rows, :HD] - top) * factor)
                hi = jnp.exp2((s_ref[g, p, rows, HD:] - top) * factor)
                s_ref[g, p, rows, :HD] = lo
                s_ref[g, p, rows, HD:] = hi
                acc_ref[g, rows] += lo + hi
        return carry

    lax.fori_loop(0, PAIRS, exp_step, 0)

    for g in range(2):
        for h in range(group):
            rows = slice(h * ROWS, (h + 1) * ROWS)
            total = jnp.sum(acc_ref[g, rows], axis=1, keepdims=True)
            stat_ref[g, rows] = jnp.broadcast_to(1.0 / total, (ROWS, HD))
        acc_ref[g] = jnp.zeros((group * ROWS, HD), F32)

    def out_step(p, carry):
        for g in range(2):
            inverse = stat_ref[g]
            lo = (s_ref[g, p, :, :HD] * inverse).astype(BF16)
            hi = (s_ref[g, p, :, HD:] * inverse).astype(BF16)
            weights = jnp.concatenate([lo, hi], axis=1)
            w_ref[g, p] = weights
            values = vbuf[window(p), g * HD : (g + 1) * HD]
            acc_ref[g] += lax.dot_general(weights, values, nn, preferred_element_type=F32)
        return carry

    lax.fori_loop(0, PAIRS, out_step, 0)

    for g in range(2):
        for h in range(group):
            rows = slice(h * ROWS, (h + 1) * ROWS)
            attended = acc_ref[g, rows].astype(BF16)
            at = (g * group + h) * HD
            att_ref[:, at : at + HD] = attended
            delta = jnp.sum(
                dos[g, rows].astype(F32) * attended.astype(F32), axis=1, keepdims=True
            )
            stat_ref[g, rows] = jnp.broadcast_to(delta, (ROWS, HD))
        acc_ref[g] = jnp.zeros((group * ROWS, HD), F32)

    load(att_ref, att_hbm, 4)
    _, at_0, _ = peer(*stages[0], 1)

    def dscore_step(p, carry):
        for g in range(2):
            keys = kbuf[window(p), g * HD : (g + 1) * HD]
            delta = stat_ref[g]
            lo = w_ref[g, p, :, :HD].astype(F32) * (p_ref[g, p, :, :HD] - delta)
            hi = w_ref[g, p, :, HD:].astype(F32) * (p_ref[g, p, :, HD:] - delta)
            dscore = jnp.concatenate([lo.astype(BF16), hi.astype(BF16)], axis=1)
            ds_ref[g, p] = dscore
            acc_ref[g] += lax.dot_general(dscore, keys, nn, preferred_element_type=F32)
        return carry

    lax.fori_loop(0, PAIRS, dscore_step, 0)
    for h in range(heads):
        g, r = h // group, (h % group) * ROWS
        cols = slice(h * HD, (h + 1) * HD)
        before = rope_back(scale * acc_ref[g, r : r + ROWS])
        gq_ref[:, cols] = before.astype(BF16)
        bst[0, at_0, h : h + 1, :] = jnp.sum(before, axis=0, keepdims=True)
    pad = bst.shape[2] - heads
    if pad:
        bst[0, at_0, heads:, :] = jnp.zeros((pad, HD), F32)
    load(gq_ref, gq_hbm, 5)

    def bias_start(i):
        kind, size = stages[i]
        for step in range(1, size):
            target, at, _ = peer(kind, size, step)
            send(c >= 0, bst.at[i, at], bst.at[i, at], brecv.at[i, at], target)

    def bias_end(i):
        kind, size = stages[i]
        for step in range(1, size):
            _, _, other = peer(kind, size, step)
            arrived(c >= 0, bst.at[i, other], brecv.at[i, other])
        total = bst[i, 0]
        for j in range(1, size):
            total = total + bst[i, j]
        if i + 1 < len(stages):
            _, at, _ = peer(*stages[i + 1], 1)
            bst[i + 1, at] = total
            bias_start(i + 1)
        else:
            total = total * (1.0 / math.sqrt(dp_size * SIDE * SIDE * ROWS))
            for h in range(heads):
                bg_ref[h * HD : (h + 1) * HD] = total[h]

    bias_start(0)

    def term_step(p, carry):
        for g in range(2):
            cols = slice(g * HD, (g + 1) * HD)
            key_term = lax.dot_general(ds_ref[g, p], qs[g], tn, preferred_element_type=F32)
            value_term = lax.dot_general(w_ref[g, p], dos[g], tn, preferred_element_type=F32)
            gkb[window(p), cols] = (scale * key_term).astype(BF16)
            gvb[window(p), cols] = value_term.astype(BF16)
        return carry

    def back_far(dr):
        so = first(dr) + xo
        pred = (z >= dr) & need(dr, x, xo)
        to_k, to_v = (left, right) if far_path(dr) else (base + xo, base + xo)
        send(pred, slot(gkb, so), far_k.at[dr], rrecv.at[dr, 0], to_k)
        send(pred, slot(gvb, so), far_v.at[dr], rrecv.at[dr, 1], to_v)

    def add_into(buf, s, other):
        rows = pl.ds(pl.multiple_of(s * ROWS, ROWS), ROWS)
        buf[rows, :] = (buf[rows, :].astype(F32) + other[...].astype(F32)).astype(BF16)

    def back_near(dr):
        valid = z >= dr
        sl, sr = first(dr) + xl, first(dr) + xr
        to_l, to_r = valid & need(dr, x, xl), valid & need(dr, x, xr)
        send(to_l, slot(gvb, sl), nr_v.at[dr], rrecv.at[dr, 3], left)
        send(to_r, slot(gkb, sr), nl_k.at[dr], rrecv.at[dr, 4], right)
        if not far_path(dr):
            send(to_l, slot(gkb, sl), nr_k.at[dr], rrecv.at[dr, 2], left)
            send(to_r, slot(gvb, sr), nl_v.at[dr], rrecv.at[dr, 5], right)
            return
        got = valid & need(dr, xr, xl)
        arrived(got, far_k.at[dr], rrecv.at[dr, 0])

        @pl.when(got)
        def _():
            add_into(gkb, sl, far_k.at[dr])

        send(to_l | got, slot(gkb, sl), nr_k.at[dr], rrecv.at[dr, 2], left)
        got_v = valid & need(dr, xl, xr)
        arrived(got_v, far_v.at[dr], rrecv.at[dr, 1])

        @pl.when(got_v)
        def _():
            add_into(gvb, sr, far_v.at[dr])

        send(to_r | got_v, slot(gvb, sr), nl_v.at[dr], rrecv.at[dr, 5], right)

    def add_when(pred, acc, src, sem):
        arrived(pred, src, sem)

        @pl.when(pred)
        def _():
            acc[...] += src[...].astype(F32)

    def back_sum(dr):
        valid = z >= dr
        so = pl.ds(pl.multiple_of((first(dr) + x) * ROWS, ROWS), ROWS)
        acck[...] = gkb[so, :].astype(F32)
        accv[...] = gvb[so, :].astype(F32)
        near_l, near_r, far = need(dr, xl, x), need(dr, xr, x), need(dr, xo, x)
        add_when(valid & near_r, accv, nr_v.at[dr], rrecv.at[dr, 3])
        add_when(valid & near_l, acck, nl_k.at[dr], rrecv.at[dr, 4])
        passed = far & far_path(dr)
        add_when(valid & (near_r | passed), acck, nr_k.at[dr], rrecv.at[dr, 2])
        add_when(valid & (near_l | passed), accv, nl_v.at[dr], rrecv.at[dr, 5])
        if not far_path(dr):
            add_when(valid & far, acck, far_k.at[dr], rrecv.at[dr, 0])
            add_when(valid & far, accv, far_v.at[dr], rrecv.at[dr, 1])
        if dr:
            zs_k[dr - 1] = acck[...].astype(BF16)
            zs_v[dr - 1] = accv[...].astype(BF16)
            down = c - SIDE * dr
            send(valid, zs_k.at[dr - 1], rz_k.at[dr - 1], rrecv.at[dr, 6], down)
            send(valid, zs_v.at[dr - 1], rz_v.at[dr - 1], rrecv.at[dr, 7], down)

    begin_pair = jnp.where(x < 2, 2, 1)
    lax.fori_loop(0, 3, lambda i, carry: term_step(begin_pair + i, carry), 0)
    back_far(1)
    end_pair = jnp.where(x < 2, 1, PAIRS - 1)
    lax.fori_loop(0, 2, lambda i, carry: term_step(i * end_pair, carry), 0)
    back_far(0)
    back_far(2)
    back_near(2)
    send(special_to, slot(gkb, 0), sp_k, rrecv.at[0, 6], c - 9)
    send(special_to, slot(gvb, 0), sp_v, rrecv.at[0, 7], c - 9)
    back_near(1)
    bias_end(0)
    back_near(0)
    back_sum(2)
    if len(stages) > 2:
        bias_end(1)
    back_sum(1)
    back_sum(0)
    for dr in (2, 1):
        add_when(z + dr < SIDE, acck, rz_k.at[dr - 1], rrecv.at[dr, 6])
        add_when(z + dr < SIDE, accv, rz_v.at[dr - 1], rrecv.at[dr, 7])
    add_when(special_from, acck, sp_k, rrecv.at[0, 6])
    add_when(special_from, accv, sp_v, rrecv.at[0, 7])
    for g in range(2):
        cols = slice(g * HD, (g + 1) * HD)
        gk_ref[:, cols] = rope_back(acck[:, cols]).astype(BF16)
    gv_ref[...] = accv[...].astype(BF16)
    load(gk_ref, gk_hbm, 6)
    load(gv_ref, gv_hbm, 7)
    bias_end(len(stages) - 1)
    loaded(att_ref, att_hbm, 4)
    loaded(gq_ref, gq_hbm, 5)
    loaded(gk_ref, gk_hbm, 6)
    loaded(gv_ref, gv_hbm, 7)

    for pred, copy in pending:

        @pl.when(pred)
        def _():
            copy.wait_send()


def write_out(*refs):
    sems = refs[-1]
    copies = [pltpu.make_async_copy(refs[i], refs[5 + i], sems.at[i]) for i in range(5)]
    for copy in copies:
        copy.start()
    for copy in copies:
        copy.wait()


def shards(q_lin, k_lin, v_lin, out_grad, q_bias, doc_lengths):
    width = q_lin.shape[2]
    heads = width // HD
    group = heads // 2
    dp_size = lax.axis_size("dp")
    exponent = np.arange(HD // 2, dtype=np.float32) * np.float32(2.0 / HD)
    freq = np.power(np.float32(THETA), -exponent).astype(np.float32)
    freq = jnp.asarray(np.concatenate([freq, freq])[None, :])
    rows = group * ROWS
    anywhere = pl.BlockSpec(memory_space=pl.ANY)
    vmem = pl.BlockSpec(memory_space=pltpu.VMEM)
    block = lambda *lead: pltpu.VMEM((*lead, ROWS, 2 * HD), BF16)
    n_stage = len(bias_stages(dp_size))
    pad_heads = -(-heads // 8) * 8
    outs = pl.pallas_call(
        lambda *refs: kernel(dp_size, group, *refs),
        out_shape=(
            jax.ShapeDtypeStruct((ROWS, width), BF16),
            jax.ShapeDtypeStruct((ROWS, width), BF16),
            jax.ShapeDtypeStruct((ROWS, 2 * HD), BF16),
            jax.ShapeDtypeStruct((ROWS, 2 * HD), BF16),
            jax.ShapeDtypeStruct((width,), F32),
        ),
        in_specs=[anywhere] * 4 + [vmem, pl.BlockSpec(memory_space=pltpu.SMEM), vmem],
        out_specs=(anywhere,) * 4 + (vmem,),
        scratch_shapes=[
            pltpu.VMEM((ROWS, width), BF16), block(), block(), pltpu.VMEM((ROWS, width), BF16),
            pltpu.VMEM((ROWS, width), BF16), pltpu.VMEM((ROWS, width), BF16), block(), block(),
            pltpu.VMEM((SLOTS * ROWS, 2 * HD), BF16),
            pltpu.VMEM((SLOTS * ROWS, 2 * HD), BF16),
            pltpu.VMEM((2, rows, HD), BF16),
            pltpu.VMEM((2, rows, HD), BF16),
            pltpu.VMEM((2, PAIRS, rows, 2 * ROWS), F32),
            pltpu.VMEM((2, PAIRS, rows, 2 * ROWS), F32),
            pltpu.VMEM((2, PAIRS, rows, 2 * ROWS), BF16),
            pltpu.VMEM((2, PAIRS, rows, 2 * ROWS), BF16),
            pltpu.VMEM((2, rows, HD), F32),
            pltpu.VMEM((2, rows, HD), F32),
            pltpu.VMEM((2, rows, HD), F32),
            pltpu.VMEM((SLOTS * ROWS, 2 * HD), BF16),
            pltpu.VMEM((SLOTS * ROWS, 2 * HD), BF16),
            block(3), block(3), block(3), block(3), block(3), block(3),
            block(2), block(2), block(2), block(2), block(), block(),
            pltpu.VMEM((ROWS, 2 * HD), F32),
            pltpu.VMEM((ROWS, 2 * HD), F32),
            pltpu.VMEM((n_stage, SIDE * SIDE, pad_heads, HD), F32),
            pltpu.VMEM((ROWS, HD), F32),
            pltpu.VMEM((ROWS, HD), F32),
            pltpu.VMEM((ROWS, HD), jnp.int32),
            pltpu.SemaphoreType.DMA((96,)),
            pltpu.SemaphoreType.DMA((SLOTS,)),
            pltpu.SemaphoreType.DMA((SLOTS,)),
            pltpu.SemaphoreType.DMA((3, 8)),
            pltpu.SemaphoreType.DMA((n_stage, SIDE * SIDE)),
            pltpu.SemaphoreType.DMA((8,)),
        ],
        compiler_params=pltpu.CompilerParams(
            collective_id=0, has_side_effects=True, vmem_limit_bytes=56 * 1024 * 1024
        ),
        cost_estimate=pl.CostEstimate(
            flops=12 * heads * ROWS * WINDOW * ROWS * HD,
            bytes_accessed=4 * 2 * ROWS * width,
            transcendentals=heads * ROWS * WINDOW * ROWS,
        ),
    )(
        q_lin.reshape(ROWS, width), k_lin.reshape(ROWS, 2 * HD), v_lin.reshape(ROWS, 2 * HD),
        out_grad.reshape(ROWS, width), q_bias, doc_lengths, freq,
    )
    attended, grad_q, grad_k, grad_v, bias_grad = pl.pallas_call(
        write_out,
        out_shape=tuple(jax.ShapeDtypeStruct(o.shape, o.dtype) for o in outs),
        in_specs=[vmem] * 5,
        out_specs=(anywhere,) * 5,
        scratch_shapes=[pltpu.SemaphoreType.DMA((5,))],
    )(*outs)
    return (attended[None], grad_q[None], grad_k[None], grad_v[None], bias_grad)


def solution(mesh):
    rows = P("dp", "ctx", None)
    return jax.shard_map(
        shards,
        mesh=mesh,
        in_specs=(rows, rows, rows, rows, P(), P("dp", None)),
        out_specs=(rows, rows, rows, rows, P()),
        check_vma=False,
    )
```

```python
import math

import jax
import jax.numpy as jnp
import numpy as np
from jax import lax
from jax.experimental import pallas as pl
from jax.experimental.pallas import tpu as pltpu
from jax.sharding import PartitionSpec as P

HD = 128
ROWS = 128
SIDE = 4
WINDOW = 10
SLOTS = 13
PAIRS = WINDOW // 2
THETA = 1000000.0
FILL = -1e30
MESH = pl.DeviceIdType.MESH
F32 = jnp.float32
BF16 = jnp.bfloat16


def bias_stages(dp_size):
    if dp_size == 32:
        return [("z", 4 * SIDE), ("x", SIDE), ("yc", 2 * SIDE)]
    return [("z", SIDE), ("x", SIDE)]


def need(dr, reader, col):
    if dr == 0:
        return col < reader
    if dr == 1:
        return col >= 0
    return col >= reader - 1


def kernel(
    dp_size, group, q_hbm, k_hbm, v_hbm, do_hbm, bias_ref, len_ref, freq_ref,
    att_ref, gq_ref, gk_ref, gv_ref, bg_ref,
    q_ref, k_ref, v_ref, do_ref,
    kbuf, vbuf, qs, dos, s_ref, p_ref, w_ref, ds_ref, acc_ref,
    gkb, gvb, far_k, far_v, nl_k, nl_v, nr_k, nr_v, rz_k, rz_v, zs_k, zs_v, sp_k, sp_v,
    acck, accv, bst, cos_ref, sin_ref, start_ref,
    send_sems, krecv, vrecv, rrecv, brecv, local_sems,
):
    c = lax.axis_index("ctx")
    d = lax.axis_index("dp")
    x = lax.rem(c, SIDE)
    z = lax.div(c, SIDE)
    base = z * SIDE
    xr, xl, xo = lax.rem(x + 1, SIDE), lax.rem(x + 3, SIDE), lax.rem(x + 2, SIDE)
    right, left = base + xr, base + xl
    scale = 1.0 / math.sqrt(HD)
    heads = 2 * group
    special_from, special_to = c == 3, c == 12

    def load(src, dst, i):
        pltpu.make_async_copy(src, dst, local_sems.at[i]).start()

    def loaded(src, dst, i):
        pltpu.make_async_copy(src, dst, local_sems.at[i]).wait()

    barrier = pltpu.get_barrier_semaphore()
    stages = bias_stages(dp_size)

    def peer(kind, size, step):
        if kind == "x":
            other = lax.rem(x + step, SIDE)
            return {"ctx": base + other}, x, other
        if kind == "z":
            high = lax.rem(lax.div(d, 2), SIDE) if size > SIDE else 0
            at = high * SIDE + z
            other = lax.rem(at + step, size)
            ctx = lax.rem(other, SIDE) * SIDE + x
            return {"dp": d + (lax.div(other, SIDE) - high) * 2, "ctx": ctx}, at, other
        y, core = lax.div(d, 8), lax.rem(d, 2)
        at = y * 2 + core
        other = lax.rem(at + step, size)
        move = (lax.div(other, 2) - y) * 8 + lax.rem(other, 2) - core
        return {"dp": d + move}, at, other

    count = jnp.where(special_from | special_to, 1, 0)
    for kind, size in stages:
        for step in range(1, size):
            target, _, _ = peer(kind, size, step)
            pl.semaphore_signal(barrier, inc=1, device_id=target, device_id_type=MESH)
        count = count + (size - 1)

    @pl.when(special_from)
    def _():
        pl.semaphore_signal(barrier, inc=1, device_id={"ctx": c + 9}, device_id_type=MESH)

    @pl.when(special_to)
    def _():
        pl.semaphore_signal(barrier, inc=1, device_id={"ctx": c - 9}, device_id_type=MESH)

    load(q_hbm, q_ref, 0)
    load(do_hbm, do_ref, 1)
    load(k_hbm, k_ref, 2)
    load(v_hbm, v_ref, 3)
    pending = []

    def slot(buf, s, blocks=1):
        return buf.at[pl.ds(pl.multiple_of(s * ROWS, ROWS), blocks * ROWS)]

    def send(pred, src, dst, recv_sem, target):
        target = target if isinstance(target, dict) else {"ctx": target}
        copy = pltpu.make_async_remote_copy(
            src_ref=src, dst_ref=dst, send_sem=send_sems.at[len(pending)], recv_sem=recv_sem,
            device_id=target, device_id_type=MESH,
        )
        pending.append((pred, copy))

        @pl.when(pred)
        def _():
            copy.start()

    def arrived(pred, dst, recv_sem):
        copy = pltpu.make_async_remote_copy(
            src_ref=dst, dst_ref=dst, send_sem=send_sems.at[0], recv_sem=recv_sem,
            device_id={"ctx": right}, device_id_type=MESH,
        )

        @pl.when(pred)
        def _():
            copy.wait_recv()

    def first(dr):
        return 9 - SIDE * dr

    def far_path(dr):
        return dr != 2

    def spread(buf, recv, is_key, dr):
        valid = z >= dr
        s = first(dr) + x
        own, sem = slot(buf, s), recv.at[s]
        if dr:
            arrived(valid, own, sem)
        if dr < 2:
            up = slot(buf, s - SIDE)
            send(valid & (z < SIDE - 1), own, up, recv.at[s - SIDE], c + SIDE)
        far = need(dr, xo, x)
        if not far_path(dr):
            send(valid & far, own, own, sem, base + xo)
        to_right, to_left = need(dr, xr, x), need(dr, xl, x)
        on_right, on_left = far_path(dr) & is_key, far_path(dr) & (not is_key)
        send(valid & (to_right | far if on_right else to_right), own, own, sem, right)
        send(valid & (to_left | far if on_left else to_left), own, own, sem, left)
        if dr == 0:
            send(special_from, own, slot(buf, 0), recv.at[0], c + 9)

    def forward_keys(dr):
        valid = z >= dr
        sl, sr = first(dr) + xl, first(dr) + xr
        kl, kr = slot(kbuf, sl), slot(kbuf, sr)
        use_l, use_r = need(dr, x, xl), need(dr, x, xr)
        on = need(dr, xr, xl) & far_path(dr)
        arrived(valid & (use_l | on), kl, krecv.at[sl])
        if far_path(dr):
            send(valid & on, kl, kl, krecv.at[sl], right)
        arrived(valid & use_r, kr, krecv.at[sr])

    def forward_values(dr):
        valid = z >= dr
        sl, sr = first(dr) + xl, first(dr) + xr
        vl, vr = slot(vbuf, sl), slot(vbuf, sr)
        use_l, use_r = need(dr, x, xl), need(dr, x, xr)
        on = need(dr, xl, xr) & far_path(dr)
        arrived(valid & (use_r | on), vr, vrecv.at[sr])
        if far_path(dr):
            send(valid & on, vr, vr, vrecv.at[sr], left)
        arrived(valid & use_l, vl, vrecv.at[sl])

    def last(buf, recv):
        for dr in (0, 1, 2):
            so = first(dr) + xo
            arrived((z >= dr) & need(dr, x, xo), slot(buf, so), recv.at[so])

    pos = c * ROWS + lax.broadcasted_iota(jnp.int32, (ROWS, HD), 0)
    start = jnp.zeros((ROWS, HD), jnp.int32)
    end = jnp.int32(0)
    for i in range(len_ref.shape[1]):
        length = len_ref[0, i]
        end = end + length
        start = start + jnp.where(end <= pos, length, 0)
    start_ref[...] = start
    angle = (pos - start).astype(F32) * freq_ref[...]
    lane = lax.broadcasted_iota(jnp.int32, (ROWS, HD), 1)
    cos_ref[...] = jnp.cos(angle)
    sine = jnp.sin(angle)
    sin_ref[...] = jnp.where(lane < HD // 2, -sine, sine)

    def rope(value):
        return value * cos_ref[...] + pltpu.roll(value, HD // 2, 1) * sin_ref[...]

    def rope_back(value):
        return value * cos_ref[...] - pltpu.roll(value, HD // 2, 1) * sin_ref[...]

    loaded(k_hbm, k_ref, 2)
    own_rows = pl.ds(pl.multiple_of((9 + x) * ROWS, ROWS), ROWS)
    for g in range(2):
        cols = slice(g * HD, (g + 1) * HD)
        kbuf[own_rows, cols] = rope(k_ref[:, cols].astype(F32)).astype(BF16)
    loaded(v_hbm, v_ref, 3)
    vbuf[own_rows, :] = v_ref[...]

    def clear(s):
        rows = pl.ds(pl.multiple_of(s * ROWS, ROWS), ROWS)
        kbuf[rows, :] = jnp.zeros((ROWS, 2 * HD), BF16)
        vbuf[rows, :] = jnp.zeros((ROWS, 2 * HD), BF16)

    for dr in (1, 2):

        @pl.when(z < dr)
        def _():
            for i in range(SIDE):
                clear(jnp.int32(first(dr) + i))

    @pl.when(c != 12)
    def _():
        clear(jnp.int32(0))

    @pl.when(x == 0)
    def _():
        gvb[10 * ROWS : 11 * ROWS, :] = jnp.zeros((ROWS, 2 * HD), BF16)

    loaded(q_hbm, q_ref, 0)
    loaded(do_hbm, do_ref, 1)
    for h in range(heads):
        g, r = h // group, (h % group) * ROWS
        cols = slice(h * HD, (h + 1) * HD)
        qs[g, r : r + ROWS, :] = rope(q_ref[:, cols].astype(F32) + bias_ref[cols]).astype(BF16)
        dos[g, r : r + ROWS, :] = do_ref[:, cols]

    nt = (((1,), (1,)), ((), ()))
    tn = (((0,), (0,)), ((), ()))
    nn = (((1,), (0,)), ((), ()))

    def window(p):
        return pl.ds(pl.multiple_of((x + 2 * p) * ROWS, ROWS), 2 * ROWS)

    first_key = (c - (WINDOW - 1)) * ROWS

    def pair_cols(p):
        return pl.ds(pl.multiple_of(p * 2 * ROWS, 2 * ROWS), 2 * ROWS)

    def score_step(p):
        key_pos = first_key + p * 2 * ROWS + lax.broadcasted_iota(jnp.int32, (ROWS, 2 * ROWS), 1)
        row = c * ROWS + lax.broadcasted_iota(jnp.int32, (ROWS, 2 * ROWS), 0)
        begin = jnp.concatenate([start_ref[...], start_ref[...]], axis=1)
        visible = (key_pos <= row) & (key_pos >= begin)
        for g in range(2):
            keys = kbuf[window(p), g * HD : (g + 1) * HD]
            raw = lax.dot_general(qs[g], keys, nt, preferred_element_type=F32)
            for h in range(group):
                rows = slice(h * ROWS, (h + 1) * ROWS)
                s_ref[g, rows, pair_cols(p)] = jnp.where(visible, raw[rows], FILL)
        return 0

    def prob_step(p):
        for g in range(2):
            values = vbuf[window(p), g * HD : (g + 1) * HD]
            p_ref[g, :, pair_cols(p)] = lax.dot_general(
                dos[g], values, nt, preferred_element_type=F32
            )
        return 0

    pl.semaphore_wait(barrier, count)
    spread(kbuf, krecv, True, 0)
    spread(vbuf, vrecv, False, 0)
    spread(kbuf, krecv, True, 1)
    forward_keys(0)
    spread(vbuf, vrecv, False, 1)
    forward_values(0)
    spread(kbuf, krecv, True, 2)
    forward_keys(1)
    spread(vbuf, vrecv, False, 2)
    forward_values(1)
    score_step(4)
    forward_keys(2)
    arrived(special_to, slot(kbuf, 0), krecv.at[0])
    lax.fori_loop(0, 2, lambda i, carry: score_step(2 - 2 * i), 0)
    prob_step(4)
    last(kbuf, krecv)
    lax.fori_loop(0, 2, lambda i, carry: score_step(3 - 2 * i), 0)

    factor = scale * math.log2(math.e)

    whole = pl.ds(pl.multiple_of(x * ROWS, ROWS), WINDOW * ROWS)
    chunk = ROWS // 4

    def softmax_step(h, carry):
        for g in range(2):
            for r in range(4):
                rows = pl.ds(pl.multiple_of(h * ROWS, ROWS) + r * chunk, chunk)
                scores = s_ref[g, rows, :]
                top = jnp.max(scores, axis=1, keepdims=True)
                terms = jnp.exp2((scores - top) * factor)
                total = jnp.sum(terms, axis=1, keepdims=True)
                w_ref[g, rows, :] = (terms * (1.0 / total)).astype(BF16)
        return carry

    lax.fori_loop(0, group, softmax_step, 0)
    forward_values(2)
    arrived(special_to, slot(vbuf, 0), vrecv.at[0])
    last(vbuf, vrecv)
    lax.fori_loop(0, PAIRS - 1, lambda p, carry: prob_step(p), 0)
    for g in range(2):
        values = vbuf[whole, g * HD : (g + 1) * HD]
        acc_ref[g] = lax.dot_general(w_ref[g], values, nn, preferred_element_type=F32)

    _, at_0, _ = peer(*stages[0], 1)

    def dscore_step(h, carry):
        for g in range(2):
            cols = pl.ds(pl.multiple_of((g * group + h) * HD, HD), HD)
            for r in range(4):
                rows = pl.ds(pl.multiple_of(h * ROWS, ROWS) + r * chunk, chunk)
                attended = acc_ref[g, rows, :].astype(BF16)
                att_ref[r * chunk : (r + 1) * chunk, cols] = attended
                product = dos[g, rows, :].astype(F32) * attended.astype(F32)
                delta = jnp.sum(product, axis=1, keepdims=True)
                weights = w_ref[g, rows, :].astype(F32)
                ds_ref[g, rows, :] = (weights * (p_ref[g, rows, :] - delta)).astype(BF16)
        return carry

    lax.fori_loop(0, group, dscore_step, 0)
    def bias_start(i):
        kind, size = stages[i]
        for step in range(1, size):
            target, at, _ = peer(kind, size, step)
            send(c >= 0, bst.at[i, at], bst.at[i, at], brecv.at[i, at], target)

    def bias_end(i):
        kind, size = stages[i]
        for step in range(1, size):
            _, _, other = peer(kind, size, step)
            arrived(c >= 0, bst.at[i, other], brecv.at[i, other])
        total = bst[i, 0]
        for j in range(1, size):
            total = total + bst[i, j]
        if i + 1 < len(stages):
            _, at, _ = peer(*stages[i + 1], 1)
            bst[i + 1, at] = total
            bias_start(i + 1)
        else:
            total = total * (1.0 / math.sqrt(dp_size * SIDE * SIDE * ROWS))
            for h in range(heads):
                bg_ref[h * HD : (h + 1) * HD] = total[h]

    def term_step(p, carry):
        for g in range(2):
            cols = slice(g * HD, (g + 1) * HD)
            key_term = lax.dot_general(
                ds_ref[g, :, pair_cols(p)], qs[g], tn, preferred_element_type=F32
            )
            value_term = lax.dot_general(
                w_ref[g, :, pair_cols(p)], dos[g], tn, preferred_element_type=F32
            )
            gkb[window(p), cols] = (scale * key_term).astype(BF16)
            gvb[window(p), cols] = value_term.astype(BF16)
        return carry

    def back_far(dr):
        so = first(dr) + xo
        pred = (z >= dr) & need(dr, x, xo)
        to_k, to_v = (left, right) if far_path(dr) else (base + xo, base + xo)
        send(pred, slot(gkb, so), far_k.at[dr], rrecv.at[dr, 0], to_k)
        send(pred, slot(gvb, so), far_v.at[dr], rrecv.at[dr, 1], to_v)

    def add_into(buf, s, other):
        rows = pl.ds(pl.multiple_of(s * ROWS, ROWS), ROWS)
        buf[rows, :] = (buf[rows, :].astype(F32) + other[...].astype(F32)).astype(BF16)

    def back_near(dr):
        valid = z >= dr
        sl, sr = first(dr) + xl, first(dr) + xr
        to_l, to_r = valid & need(dr, x, xl), valid & need(dr, x, xr)
        send(to_l, slot(gvb, sl), nr_v.at[dr], rrecv.at[dr, 3], left)
        send(to_r, slot(gkb, sr), nl_k.at[dr], rrecv.at[dr, 4], right)
        if not far_path(dr):
            send(to_l, slot(gkb, sl), nr_k.at[dr], rrecv.at[dr, 2], left)
            send(to_r, slot(gvb, sr), nl_v.at[dr], rrecv.at[dr, 5], right)
            return
        got = valid & need(dr, xr, xl)
        arrived(got, far_k.at[dr], rrecv.at[dr, 0])

        @pl.when(got)
        def _():
            add_into(gkb, sl, far_k.at[dr])

        send(to_l | got, slot(gkb, sl), nr_k.at[dr], rrecv.at[dr, 2], left)
        got_v = valid & need(dr, xl, xr)
        arrived(got_v, far_v.at[dr], rrecv.at[dr, 1])

        @pl.when(got_v)
        def _():
            add_into(gvb, sr, far_v.at[dr])

        send(to_r | got_v, slot(gvb, sr), nl_v.at[dr], rrecv.at[dr, 5], right)

    def add_when(pred, acc, src, sem):
        arrived(pred, src, sem)

        @pl.when(pred)
        def _():
            acc[...] += src[...].astype(F32)

    def back_sum(dr):
        valid = z >= dr
        so = pl.ds(pl.multiple_of((first(dr) + x) * ROWS, ROWS), ROWS)
        acck[...] = gkb[so, :].astype(F32)
        accv[...] = gvb[so, :].astype(F32)
        near_l, near_r, far = need(dr, xl, x), need(dr, xr, x), need(dr, xo, x)
        add_when(valid & near_r, accv, nr_v.at[dr], rrecv.at[dr, 3])
        add_when(valid & near_l, acck, nl_k.at[dr], rrecv.at[dr, 4])
        passed = far & far_path(dr)
        add_when(valid & (near_r | passed), acck, nr_k.at[dr], rrecv.at[dr, 2])
        add_when(valid & (near_l | passed), accv, nl_v.at[dr], rrecv.at[dr, 5])
        if not far_path(dr):
            add_when(valid & far, acck, far_k.at[dr], rrecv.at[dr, 0])
            add_when(valid & far, accv, far_v.at[dr], rrecv.at[dr, 1])
        if dr:
            zs_k[dr - 1] = acck[...].astype(BF16)
            zs_v[dr - 1] = accv[...].astype(BF16)
            down = c - SIDE * dr
            send(valid, zs_k.at[dr - 1], rz_k.at[dr - 1], rrecv.at[dr, 6], down)
            send(valid, zs_v.at[dr - 1], rz_v.at[dr - 1], rrecv.at[dr, 7], down)

    begin_pair = jnp.where(x < 2, 2, 1)
    lax.fori_loop(0, 3, lambda i, carry: term_step(begin_pair + i, carry), 0)
    back_far(1)

    for g in range(2):
        keys = kbuf[whole, g * HD : (g + 1) * HD]
        acc_ref[g] = lax.dot_general(ds_ref[g], keys, nn, preferred_element_type=F32)
    for h in range(heads):
        g, r = h // group, (h % group) * ROWS
        cols = slice(h * HD, (h + 1) * HD)
        before = rope_back(scale * acc_ref[g, r : r + ROWS])
        gq_ref[:, cols] = before.astype(BF16)
        bst[0, at_0, h : h + 1, :] = jnp.sum(before, axis=0, keepdims=True)
    pad = bst.shape[2] - heads
    if pad:
        bst[0, at_0, heads:, :] = jnp.zeros((pad, HD), F32)
    bias_start(0)

    end_pair = jnp.where(x < 2, 1, PAIRS - 1)
    lax.fori_loop(0, 2, lambda i, carry: term_step(i * end_pair, carry), 0)
    back_far(0)
    back_far(2)
    back_near(2)
    send(special_to, slot(gkb, 0), sp_k, rrecv.at[0, 6], c - 9)
    send(special_to, slot(gvb, 0), sp_v, rrecv.at[0, 7], c - 9)
    back_near(1)
    bias_end(0)
    back_near(0)
    back_sum(2)
    if len(stages) > 2:
        bias_end(1)
    back_sum(1)
    back_sum(0)
    for dr in (2, 1):
        add_when(z + dr < SIDE, acck, rz_k.at[dr - 1], rrecv.at[dr, 6])
        add_when(z + dr < SIDE, accv, rz_v.at[dr - 1], rrecv.at[dr, 7])
    add_when(special_from, acck, sp_k, rrecv.at[0, 6])
    add_when(special_from, accv, sp_v, rrecv.at[0, 7])
    for g in range(2):
        cols = slice(g * HD, (g + 1) * HD)
        gk_ref[:, cols] = rope_back(acck[:, cols]).astype(BF16)
    gv_ref[...] = accv[...].astype(BF16)
    bias_end(len(stages) - 1)

    for pred, copy in pending:

        @pl.when(pred)
        def _():
            copy.wait_send()


def write_out(*refs):
    sems = refs[10]
    copies = [pltpu.make_async_copy(refs[i], refs[5 + i], sems.at[i]) for i in range(5)]
    for copy in copies:
        copy.start()
    for copy in copies:
        copy.wait()


def shards(q_lin, k_lin, v_lin, out_grad, q_bias, doc_lengths):
    width = q_lin.shape[2]
    heads = width // HD
    group = heads // 2
    dp_size = lax.axis_size("dp")
    exponent = np.arange(HD // 2, dtype=np.float32) * np.float32(2.0 / HD)
    freq = np.power(np.float32(THETA), -exponent).astype(np.float32)
    freq = jnp.asarray(np.concatenate([freq, freq])[None, :])
    rows = group * ROWS
    anywhere = pl.BlockSpec(memory_space=pl.ANY)
    vmem = pl.BlockSpec(memory_space=pltpu.VMEM)
    block = lambda *lead: pltpu.VMEM((*lead, ROWS, 2 * HD), BF16)
    n_stage = len(bias_stages(dp_size))
    pad_heads = -(-heads // 8) * 8
    outs = pl.pallas_call(
        lambda *refs: kernel(dp_size, group, *refs),
        out_shape=(
            pltpu.VMEM((ROWS, width), BF16),
            pltpu.VMEM((ROWS, width), BF16),
            pltpu.VMEM((ROWS, 2 * HD), BF16),
            pltpu.VMEM((ROWS, 2 * HD), BF16),
            pltpu.VMEM((width,), F32),
        ),
        in_specs=[anywhere] * 4 + [vmem, pl.BlockSpec(memory_space=pltpu.SMEM), vmem],
        out_specs=(vmem,) * 5,
        scratch_shapes=[
            pltpu.VMEM((ROWS, width), BF16), block(), block(), pltpu.VMEM((ROWS, width), BF16),
            pltpu.VMEM((SLOTS * ROWS, 2 * HD), BF16),
            pltpu.VMEM((SLOTS * ROWS, 2 * HD), BF16),
            pltpu.VMEM((2, rows, HD), BF16),
            pltpu.VMEM((2, rows, HD), BF16),
            pltpu.VMEM((2, rows, WINDOW * ROWS), F32),
            pltpu.VMEM((2, rows, WINDOW * ROWS), F32),
            pltpu.VMEM((2, rows, WINDOW * ROWS), BF16),
            pltpu.VMEM((2, rows, WINDOW * ROWS), BF16),
            pltpu.VMEM((2, rows, HD), F32),
            pltpu.VMEM((SLOTS * ROWS, 2 * HD), BF16),
            pltpu.VMEM((SLOTS * ROWS, 2 * HD), BF16),
            block(3), block(3), block(3), block(3), block(3), block(3),
            block(2), block(2), block(2), block(2), block(), block(),
            pltpu.VMEM((ROWS, 2 * HD), F32),
            pltpu.VMEM((ROWS, 2 * HD), F32),
            pltpu.VMEM((n_stage, SIDE * SIDE, pad_heads, HD), F32),
            pltpu.VMEM((ROWS, HD), F32),
            pltpu.VMEM((ROWS, HD), F32),
            pltpu.VMEM((ROWS, HD), jnp.int32),
            pltpu.SemaphoreType.DMA((96,)),
            pltpu.SemaphoreType.DMA((SLOTS,)),
            pltpu.SemaphoreType.DMA((SLOTS,)),
            pltpu.SemaphoreType.DMA((3, 8)),
            pltpu.SemaphoreType.DMA((n_stage, SIDE * SIDE)),
            pltpu.SemaphoreType.DMA((8,)),
        ],
        compiler_params=pltpu.CompilerParams(
            collective_id=0, has_side_effects=True, vmem_limit_bytes=56 * 1024 * 1024
        ),
        cost_estimate=pl.CostEstimate(
            flops=12 * heads * ROWS * WINDOW * ROWS * HD,
            bytes_accessed=4 * 2 * ROWS * width,
            transcendentals=heads * ROWS * WINDOW * ROWS,
        ),
    )(
        q_lin.reshape(ROWS, width), k_lin.reshape(ROWS, 2 * HD), v_lin.reshape(ROWS, 2 * HD),
        out_grad.reshape(ROWS, width), q_bias, doc_lengths, freq,
    )
    attended, grad_q, grad_k, grad_v, bias_grad = pl.pallas_call(
        write_out,
        out_shape=tuple(jax.ShapeDtypeStruct(o.shape, o.dtype) for o in outs),
        in_specs=[vmem] * 5,
        out_specs=(anywhere,) * 5,
        scratch_shapes=[pltpu.SemaphoreType.DMA((5,))],
    )(*(pltpu.with_memory_space_constraint(o, pltpu.VMEM) for o in outs))
    return (attended[None], grad_q[None], grad_k[None], grad_v[None], bias_grad)


def solution(mesh):
    rows = P("dp", "ctx", None)
    return jax.shard_map(
        shards,
        mesh=mesh,
        in_specs=(rows, rows, rows, rows, P(), P("dp", None)),
        out_specs=(rows, rows, rows, rows, P()),
        check_vma=False,
    )
```

```python
import math

import jax
import jax.numpy as jnp
import numpy as np
from jax import lax
from jax.experimental import pallas as pl
from jax.experimental.pallas import tpu as pltpu
from jax.sharding import PartitionSpec as P

HD = 128
ROWS = 128
SIDE = 4
NEAR = 4
WINDOW = 10
SLOTS = 13
PAIRS = WINDOW // 2
THETA = 1000000.0
FILL = -1e30
MESH = pl.DeviceIdType.MESH
F32 = jnp.float32
BF16 = jnp.bfloat16


def bias_stages(dp_size):
    if dp_size == 32:
        return [("z", 4 * SIDE), ("x", SIDE), ("yc", 2 * SIDE)]
    return [("z", SIDE), ("x", SIDE)]


def need(dr, reader, col):
    if dr == 0:
        return col < reader
    if dr == 1:
        return col >= 0
    return col >= reader - 1


def kernel(
    dp_size, group, q_hbm, k_hbm, v_hbm, do_hbm, bias_ref, len_ref, freq_ref,
    att_ref, gq_ref, gk_ref, gv_ref, bg_ref,
    q_ref, k_ref, v_ref, do_ref,
    kbuf, vbuf, qs, dos, s_ref, p_ref, w_ref, ds_ref, acc_ref,
    gkb, gvb, far_k, far_v, nl_k, nl_v, nr_k, nr_v, rz_k, rz_v, zs_k, zs_v, sp_k, sp_v,
    acck, accv, bst, cos_ref, sin_ref, start_ref,
    send_sems, krecv, vrecv, rrecv, brecv, local_sems, relay_sem,
):
    c = lax.axis_index("ctx")
    d = lax.axis_index("dp")
    x = lax.rem(c, SIDE)
    z = lax.div(c, SIDE)
    base = z * SIDE
    xr, xl, xo = lax.rem(x + 1, SIDE), lax.rem(x + 3, SIDE), lax.rem(x + 2, SIDE)
    right, left = base + xr, base + xl
    scale = 1.0 / math.sqrt(HD)
    heads = 2 * group
    special_from, special_to = c == 3, c == 12

    def load(src, dst, i):
        pltpu.make_async_copy(src, dst, local_sems.at[i]).start()

    def loaded(src, dst, i):
        pltpu.make_async_copy(src, dst, local_sems.at[i]).wait()

    barrier = pltpu.get_barrier_semaphore()
    stages = bias_stages(dp_size)

    def peer(kind, size, step):
        if kind == "x":
            other = lax.rem(x + step, SIDE)
            return {"ctx": base + other}, x, other
        if kind == "z":
            high = lax.rem(lax.div(d, 2), SIDE) if size > SIDE else 0
            at = high * SIDE + z
            other = lax.rem(at + step, size)
            ctx = lax.rem(other, SIDE) * SIDE + x
            return {"dp": d + (lax.div(other, SIDE) - high) * 2, "ctx": ctx}, at, other
        y, core = lax.div(d, 8), lax.rem(d, 2)
        at = y * 2 + core
        other = lax.rem(at + step, size)
        move = (lax.div(other, 2) - y) * 8 + lax.rem(other, 2) - core
        return {"dp": d + move}, at, other

    count = jnp.where(special_from | special_to, 1, 0)
    for kind, size in stages:
        greeted = [s for s in range(1, size) if min(s, size - s) <= NEAR or kind != "z"]
        for step in greeted:
            target, _, _ = peer(kind, size, step)
            pl.semaphore_signal(barrier, inc=1, device_id=target, device_id_type=MESH)
        count = count + len(greeted)

    @pl.when(special_from)
    def _():
        pl.semaphore_signal(barrier, inc=1, device_id={"ctx": c + 9}, device_id_type=MESH)

    @pl.when(special_to)
    def _():
        pl.semaphore_signal(barrier, inc=1, device_id={"ctx": c - 9}, device_id_type=MESH)

    load(q_hbm, q_ref, 0)
    load(do_hbm, do_ref, 1)
    load(k_hbm, k_ref, 2)
    load(v_hbm, v_ref, 3)
    pending = []

    def slot(buf, s, blocks=1):
        return buf.at[pl.ds(pl.multiple_of(s * ROWS, ROWS), blocks * ROWS)]

    def send(pred, src, dst, recv_sem, target):
        target = target if isinstance(target, dict) else {"ctx": target}
        copy = pltpu.make_async_remote_copy(
            src_ref=src, dst_ref=dst, send_sem=send_sems.at[len(pending)], recv_sem=recv_sem,
            device_id=target, device_id_type=MESH,
        )
        pending.append((pred, copy))

        @pl.when(pred)
        def _():
            copy.start()

    def arrived(pred, dst, recv_sem):
        copy = pltpu.make_async_remote_copy(
            src_ref=dst, dst_ref=dst, send_sem=send_sems.at[0], recv_sem=recv_sem,
            device_id={"ctx": right}, device_id_type=MESH,
        )

        @pl.when(pred)
        def _():
            copy.wait_recv()

    def first(dr):
        return 9 - SIDE * dr

    def far_path(dr):
        return dr != 2

    def spread(buf, recv, is_key, dr):
        valid = z >= dr
        s = first(dr) + x
        own, sem = slot(buf, s), recv.at[s]
        if dr:
            arrived(valid, own, sem)
        if dr < 2:
            up = slot(buf, s - SIDE)
            send(valid & (z < SIDE - 1), own, up, recv.at[s - SIDE], c + SIDE)
        far = need(dr, xo, x)
        if not far_path(dr):
            send(valid & far, own, own, sem, base + xo)
        to_right, to_left = need(dr, xr, x), need(dr, xl, x)
        on_right, on_left = far_path(dr) & is_key, far_path(dr) & (not is_key)
        send(valid & (to_right | far if on_right else to_right), own, own, sem, right)
        send(valid & (to_left | far if on_left else to_left), own, own, sem, left)
        if dr == 0:
            send(special_from, own, slot(buf, 0), recv.at[0], c + 9)

    def forward_keys(dr):
        valid = z >= dr
        sl, sr = first(dr) + xl, first(dr) + xr
        kl, kr = slot(kbuf, sl), slot(kbuf, sr)
        use_l, use_r = need(dr, x, xl), need(dr, x, xr)
        on = need(dr, xr, xl) & far_path(dr)
        arrived(valid & (use_l | on), kl, krecv.at[sl])
        if far_path(dr):
            send(valid & on, kl, kl, krecv.at[sl], right)
        arrived(valid & use_r, kr, krecv.at[sr])

    def forward_values(dr):
        valid = z >= dr
        sl, sr = first(dr) + xl, first(dr) + xr
        vl, vr = slot(vbuf, sl), slot(vbuf, sr)
        use_l, use_r = need(dr, x, xl), need(dr, x, xr)
        on = need(dr, xl, xr) & far_path(dr)
        arrived(valid & (use_r | on), vr, vrecv.at[sr])
        if far_path(dr):
            send(valid & on, vr, vr, vrecv.at[sr], left)
        arrived(valid & use_l, vl, vrecv.at[sl])

    def last(buf, recv):
        for dr in (0, 1, 2):
            so = first(dr) + xo
            arrived((z >= dr) & need(dr, x, xo), slot(buf, so), recv.at[so])

    pos = c * ROWS + lax.broadcasted_iota(jnp.int32, (ROWS, HD), 0)
    start = jnp.zeros((ROWS, HD), jnp.int32)
    end = jnp.int32(0)
    for i in range(len_ref.shape[1]):
        length = len_ref[0, i]
        end = end + length
        start = start + jnp.where(end <= pos, length, 0)
    start_ref[...] = start
    angle = (pos - start).astype(F32) * freq_ref[...]
    lane = lax.broadcasted_iota(jnp.int32, (ROWS, HD), 1)
    cos_ref[...] = jnp.cos(angle)
    sine = jnp.sin(angle)
    sin_ref[...] = jnp.where(lane < HD // 2, -sine, sine)

    def rope(value):
        return value * cos_ref[...] + pltpu.roll(value, HD // 2, 1) * sin_ref[...]

    def rope_back(value):
        return value * cos_ref[...] - pltpu.roll(value, HD // 2, 1) * sin_ref[...]

    loaded(k_hbm, k_ref, 2)
    own_rows = pl.ds(pl.multiple_of((9 + x) * ROWS, ROWS), ROWS)
    for g in range(2):
        cols = slice(g * HD, (g + 1) * HD)
        kbuf[own_rows, cols] = rope(k_ref[:, cols].astype(F32)).astype(BF16)
    loaded(v_hbm, v_ref, 3)
    vbuf[own_rows, :] = v_ref[...]

    def clear(s):
        rows = pl.ds(pl.multiple_of(s * ROWS, ROWS), ROWS)
        kbuf[rows, :] = jnp.zeros((ROWS, 2 * HD), BF16)
        vbuf[rows, :] = jnp.zeros((ROWS, 2 * HD), BF16)

    for dr in (1, 2):

        @pl.when(z < dr)
        def _():
            for i in range(SIDE):
                clear(jnp.int32(first(dr) + i))

    @pl.when(c != 12)
    def _():
        clear(jnp.int32(0))

    @pl.when(x == 0)
    def _():
        gvb[10 * ROWS : 11 * ROWS, :] = jnp.zeros((ROWS, 2 * HD), BF16)

    loaded(q_hbm, q_ref, 0)
    loaded(do_hbm, do_ref, 1)
    for h in range(heads):
        g, r = h // group, (h % group) * ROWS
        cols = slice(h * HD, (h + 1) * HD)
        qs[g, r : r + ROWS, :] = rope(q_ref[:, cols].astype(F32) + bias_ref[cols]).astype(BF16)
        dos[g, r : r + ROWS, :] = do_ref[:, cols]

    nt = (((1,), (1,)), ((), ()))
    tn = (((0,), (0,)), ((), ()))
    nn = (((1,), (0,)), ((), ()))

    def window(p):
        return pl.ds(pl.multiple_of((x + 2 * p) * ROWS, ROWS), 2 * ROWS)

    first_key = (c - (WINDOW - 1)) * ROWS

    def pair_cols(p):
        return pl.ds(pl.multiple_of(p * 2 * ROWS, 2 * ROWS), 2 * ROWS)

    def score_step(p):
        key_pos = first_key + p * 2 * ROWS + lax.broadcasted_iota(jnp.int32, (ROWS, 2 * ROWS), 1)
        row = c * ROWS + lax.broadcasted_iota(jnp.int32, (ROWS, 2 * ROWS), 0)
        begin = jnp.concatenate([start_ref[...], start_ref[...]], axis=1)
        visible = (key_pos <= row) & (key_pos >= begin)
        for g in range(2):
            keys = kbuf[window(p), g * HD : (g + 1) * HD]
            raw = lax.dot_general(qs[g], keys, nt, preferred_element_type=F32)
            for h in range(group):
                rows = slice(h * ROWS, (h + 1) * ROWS)
                s_ref[g, rows, pair_cols(p)] = jnp.where(visible, raw[rows], FILL)
        return 0

    def prob_step(p):
        for g in range(2):
            values = vbuf[window(p), g * HD : (g + 1) * HD]
            p_ref[g, :, pair_cols(p)] = lax.dot_general(
                dos[g], values, nt, preferred_element_type=F32
            )
        return 0

    pl.semaphore_wait(barrier, count)
    kind, size = stages[0]
    relayed = size > 2 * NEAR
    if relayed:
        for step in (NEAR, size - NEAR):
            target, _, _ = peer(kind, size, step)
            pl.semaphore_signal(relay_sem, inc=1, device_id=target, device_id_type=MESH)
    spread(kbuf, krecv, True, 0)
    spread(vbuf, vrecv, False, 0)
    spread(kbuf, krecv, True, 1)
    forward_keys(0)
    spread(vbuf, vrecv, False, 1)
    forward_values(0)
    spread(kbuf, krecv, True, 2)
    forward_keys(1)
    spread(vbuf, vrecv, False, 2)
    forward_values(1)
    score_step(4)
    forward_keys(2)
    arrived(special_to, slot(kbuf, 0), krecv.at[0])
    lax.fori_loop(0, 2, lambda i, carry: score_step(2 - 2 * i), 0)
    prob_step(4)
    last(kbuf, krecv)
    lax.fori_loop(0, 2, lambda i, carry: score_step(3 - 2 * i), 0)

    factor = scale * math.log2(math.e)

    whole = pl.ds(pl.multiple_of(x * ROWS, ROWS), WINDOW * ROWS)
    chunk = ROWS // 4

    def softmax_step(h, carry):
        for g in range(2):
            for r in range(4):
                rows = pl.ds(pl.multiple_of(h * ROWS, ROWS) + r * chunk, chunk)
                scores = s_ref[g, rows, :]
                top = jnp.max(scores, axis=1, keepdims=True)
                terms = jnp.exp2((scores - top) * factor)
                total = jnp.sum(terms, axis=1, keepdims=True)
                w_ref[g, rows, :] = (terms * (1.0 / total)).astype(BF16)
        return carry

    lax.fori_loop(0, group, softmax_step, 0)
    forward_values(2)
    arrived(special_to, slot(vbuf, 0), vrecv.at[0])
    last(vbuf, vrecv)
    lax.fori_loop(0, PAIRS - 1, lambda p, carry: prob_step(p), 0)
    for g in range(2):
        values = vbuf[whole, g * HD : (g + 1) * HD]
        acc_ref[g] = lax.dot_general(w_ref[g], values, nn, preferred_element_type=F32)

    _, at_0, _ = peer(*stages[0], 1)

    def dscore_step(h, carry):
        for g in range(2):
            cols = pl.ds(pl.multiple_of((g * group + h) * HD, HD), HD)
            for r in range(4):
                rows = pl.ds(pl.multiple_of(h * ROWS, ROWS) + r * chunk, chunk)
                attended = acc_ref[g, rows, :].astype(BF16)
                att_ref[r * chunk : (r + 1) * chunk, cols] = attended
                product = dos[g, rows, :].astype(F32) * attended.astype(F32)
                delta = jnp.sum(product, axis=1, keepdims=True)
                weights = w_ref[g, rows, :].astype(F32)
                ds_ref[g, rows, :] = (weights * (p_ref[g, rows, :] - delta)).astype(BF16)
        return carry

    lax.fori_loop(0, group, dscore_step, 0)
    def bias_start(i):
        kind, size = stages[i]
        for step in range(1, size):
            target, at, _ = peer(kind, size, step)
            send(c >= 0, bst.at[i, at], bst.at[i, at], brecv.at[i, at], target)

    def bias_end(i):
        kind, size = stages[i]
        for step in range(1, size):
            _, _, other = peer(kind, size, step)
            arrived(c >= 0, bst.at[i, other], brecv.at[i, other])
        total = bst[i, 0]
        for j in range(1, size):
            total = total + bst[i, j]
        if i + 1 < len(stages):
            _, at, _ = peer(*stages[i + 1], 1)
            bst[i + 1, at] = total
            bias_start(i + 1)
        else:
            total = total * (1.0 / math.sqrt(dp_size * SIDE * SIDE * ROWS))
            for h in range(heads):
                bg_ref[h * HD : (h + 1) * HD] = total[h]

    def term_step(p, carry):
        for g in range(2):
            cols = slice(g * HD, (g + 1) * HD)
            key_term = lax.dot_general(
                ds_ref[g, :, pair_cols(p)], qs[g], tn, preferred_element_type=F32
            )
            value_term = lax.dot_general(
                w_ref[g, :, pair_cols(p)], dos[g], tn, preferred_element_type=F32
            )
            gkb[window(p), cols] = (scale * key_term).astype(BF16)
            gvb[window(p), cols] = value_term.astype(BF16)
        return carry

    def back_far(dr):
        so = first(dr) + xo
        pred = (z >= dr) & need(dr, x, xo)
        to_k, to_v = (left, right) if far_path(dr) else (base + xo, base + xo)
        send(pred, slot(gkb, so), far_k.at[dr], rrecv.at[dr, 0], to_k)
        send(pred, slot(gvb, so), far_v.at[dr], rrecv.at[dr, 1], to_v)
        valid = z >= dr
        to_l, to_r = valid & need(dr, x, xl), valid & need(dr, x, xr)
        send(to_l, slot(gvb, first(dr) + xl), nr_v.at[dr], rrecv.at[dr, 3], left)
        send(to_r, slot(gkb, first(dr) + xr), nl_k.at[dr], rrecv.at[dr, 4], right)

    def add_into(buf, s, other):
        rows = pl.ds(pl.multiple_of(s * ROWS, ROWS), ROWS)
        buf[rows, :] = (buf[rows, :].astype(F32) + other[...].astype(F32)).astype(BF16)

    def back_near(dr):
        valid = z >= dr
        sl, sr = first(dr) + xl, first(dr) + xr
        to_l, to_r = valid & need(dr, x, xl), valid & need(dr, x, xr)
        if not far_path(dr):
            send(to_l, slot(gkb, sl), nr_k.at[dr], rrecv.at[dr, 2], left)
            send(to_r, slot(gvb, sr), nl_v.at[dr], rrecv.at[dr, 5], right)
            return
        got = valid & need(dr, xr, xl)
        arrived(got, far_k.at[dr], rrecv.at[dr, 0])

        @pl.when(got)
        def _():
            add_into(gkb, sl, far_k.at[dr])

        send(to_l | got, slot(gkb, sl), nr_k.at[dr], rrecv.at[dr, 2], left)
        got_v = valid & need(dr, xl, xr)
        arrived(got_v, far_v.at[dr], rrecv.at[dr, 1])

        @pl.when(got_v)
        def _():
            add_into(gvb, sr, far_v.at[dr])

        send(to_r | got_v, slot(gvb, sr), nl_v.at[dr], rrecv.at[dr, 5], right)

    def add_when(pred, acc, src, sem):
        arrived(pred, src, sem)

        @pl.when(pred)
        def _():
            acc[...] += src[...].astype(F32)

    def back_sum(dr):
        valid = z >= dr
        so = pl.ds(pl.multiple_of((first(dr) + x) * ROWS, ROWS), ROWS)
        acck[...] = gkb[so, :].astype(F32)
        accv[...] = gvb[so, :].astype(F32)
        near_l, near_r, far = need(dr, xl, x), need(dr, xr, x), need(dr, xo, x)
        add_when(valid & near_r, accv, nr_v.at[dr], rrecv.at[dr, 3])
        add_when(valid & near_l, acck, nl_k.at[dr], rrecv.at[dr, 4])
        passed = far & far_path(dr)
        add_when(valid & (near_r | passed), acck, nr_k.at[dr], rrecv.at[dr, 2])
        add_when(valid & (near_l | passed), accv, nl_v.at[dr], rrecv.at[dr, 5])
        if not far_path(dr):
            add_when(valid & far, acck, far_k.at[dr], rrecv.at[dr, 0])
            add_when(valid & far, accv, far_v.at[dr], rrecv.at[dr, 1])
        if dr:
            zs_k[dr - 1] = acck[...].astype(BF16)
            zs_v[dr - 1] = accv[...].astype(BF16)
            down = c - SIDE * dr
            send(valid, zs_k.at[dr - 1], rz_k.at[dr - 1], rrecv.at[dr, 6], down)
            send(valid, zs_v.at[dr - 1], rz_v.at[dr - 1], rrecv.at[dr, 7], down)

    begin_pair = jnp.where(x < 2, 2, 1)
    lax.fori_loop(0, 3, lambda i, carry: term_step(begin_pair + i, carry), 0)
    back_far(1)

    for g in range(2):
        keys = kbuf[whole, g * HD : (g + 1) * HD]
        acc_ref[g] = lax.dot_general(ds_ref[g], keys, nn, preferred_element_type=F32)
    for h in range(heads):
        g, r = h // group, (h % group) * ROWS
        cols = slice(h * HD, (h + 1) * HD)
        before = rope_back(scale * acc_ref[g, r : r + ROWS])
        gq_ref[:, cols] = before.astype(BF16)
        bst[0, at_0, h : h + 1, :] = jnp.sum(before, axis=0, keepdims=True)
    pad = bst.shape[2] - heads
    if pad:
        bst[0, at_0, heads:, :] = jnp.zeros((pad, HD), F32)
    if relayed:
        pl.semaphore_wait(relay_sem, 2)
    bias_start(0)

    end_pair = jnp.where(x < 2, 1, PAIRS - 1)
    lax.fori_loop(0, 2, lambda i, carry: term_step(i * end_pair, carry), 0)
    back_far(0)
    back_far(2)
    back_near(2)
    send(special_to, slot(gkb, 0), sp_k, rrecv.at[0, 6], c - 9)
    send(special_to, slot(gvb, 0), sp_v, rrecv.at[0, 7], c - 9)
    back_near(1)
    bias_end(0)
    back_near(0)
    back_sum(2)
    back_sum(1)
    if len(stages) > 2:
        bias_end(1)
    back_sum(0)
    for dr in (2, 1):
        add_when(z + dr < SIDE, acck, rz_k.at[dr - 1], rrecv.at[dr, 6])
        add_when(z + dr < SIDE, accv, rz_v.at[dr - 1], rrecv.at[dr, 7])
    add_when(special_from, acck, sp_k, rrecv.at[0, 6])
    add_when(special_from, accv, sp_v, rrecv.at[0, 7])
    for g in range(2):
        cols = slice(g * HD, (g + 1) * HD)
        gk_ref[:, cols] = rope_back(acck[:, cols]).astype(BF16)
    gv_ref[...] = accv[...].astype(BF16)
    bias_end(len(stages) - 1)

    for pred, copy in pending:

        @pl.when(pred)
        def _():
            copy.wait_send()


def write_out(*refs):
    sems = refs[10]
    copies = [pltpu.make_async_copy(refs[i], refs[5 + i], sems.at[i]) for i in range(5)]
    for copy in copies:
        copy.start()
    for copy in copies:
        copy.wait()


def shards(q_lin, k_lin, v_lin, out_grad, q_bias, doc_lengths):
    width = q_lin.shape[2]
    heads = width // HD
    group = heads // 2
    dp_size = lax.axis_size("dp")
    exponent = np.arange(HD // 2, dtype=np.float32) * np.float32(2.0 / HD)
    freq = np.power(np.float32(THETA), -exponent).astype(np.float32)
    freq = jnp.asarray(np.concatenate([freq, freq])[None, :])
    rows = group * ROWS
    anywhere = pl.BlockSpec(memory_space=pl.ANY)
    vmem = pl.BlockSpec(memory_space=pltpu.VMEM)
    block = lambda *lead: pltpu.VMEM((*lead, ROWS, 2 * HD), BF16)
    n_stage = len(bias_stages(dp_size))
    pad_heads = -(-heads // 8) * 8
    outs = pl.pallas_call(
        lambda *refs: kernel(dp_size, group, *refs),
        out_shape=(
            pltpu.VMEM((ROWS, width), BF16),
            pltpu.VMEM((ROWS, width), BF16),
            pltpu.VMEM((ROWS, 2 * HD), BF16),
            pltpu.VMEM((ROWS, 2 * HD), BF16),
            pltpu.VMEM((width,), F32),
        ),
        in_specs=[anywhere] * 4 + [vmem, pl.BlockSpec(memory_space=pltpu.SMEM), vmem],
        out_specs=(vmem,) * 5,
        scratch_shapes=[
            pltpu.VMEM((ROWS, width), BF16), block(), block(), pltpu.VMEM((ROWS, width), BF16),
            pltpu.VMEM((SLOTS * ROWS, 2 * HD), BF16),
            pltpu.VMEM((SLOTS * ROWS, 2 * HD), BF16),
            pltpu.VMEM((2, rows, HD), BF16),
            pltpu.VMEM((2, rows, HD), BF16),
            pltpu.VMEM((2, rows, WINDOW * ROWS), F32),
            pltpu.VMEM((2, rows, WINDOW * ROWS), F32),
            pltpu.VMEM((2, rows, WINDOW * ROWS), BF16),
            pltpu.VMEM((2, rows, WINDOW * ROWS), BF16),
            pltpu.VMEM((2, rows, HD), F32),
            pltpu.VMEM((SLOTS * ROWS, 2 * HD), BF16),
            pltpu.VMEM((SLOTS * ROWS, 2 * HD), BF16),
            block(3), block(3), block(3), block(3), block(3), block(3),
            block(2), block(2), block(2), block(2), block(), block(),
            pltpu.VMEM((ROWS, 2 * HD), F32),
            pltpu.VMEM((ROWS, 2 * HD), F32),
            pltpu.VMEM((n_stage, SIDE * SIDE, pad_heads, HD), F32),
            pltpu.VMEM((ROWS, HD), F32),
            pltpu.VMEM((ROWS, HD), F32),
            pltpu.VMEM((ROWS, HD), jnp.int32),
            pltpu.SemaphoreType.DMA((96,)),
            pltpu.SemaphoreType.DMA((SLOTS,)),
            pltpu.SemaphoreType.DMA((SLOTS,)),
            pltpu.SemaphoreType.DMA((3, 8)),
            pltpu.SemaphoreType.DMA((n_stage, SIDE * SIDE)),
            pltpu.SemaphoreType.DMA((8,)),
            pltpu.SemaphoreType.REGULAR,
        ],
        compiler_params=pltpu.CompilerParams(
            collective_id=0, has_side_effects=True, vmem_limit_bytes=56 * 1024 * 1024
        ),
        cost_estimate=pl.CostEstimate(
            flops=12 * heads * ROWS * WINDOW * ROWS * HD,
            bytes_accessed=4 * 2 * ROWS * width,
            transcendentals=heads * ROWS * WINDOW * ROWS,
        ),
    )(
        q_lin.reshape(ROWS, width), k_lin.reshape(ROWS, 2 * HD), v_lin.reshape(ROWS, 2 * HD),
        out_grad.reshape(ROWS, width), q_bias, doc_lengths, freq,
    )
    attended, grad_q, grad_k, grad_v, bias_grad = pl.pallas_call(
        write_out,
        out_shape=tuple(jax.ShapeDtypeStruct(o.shape, o.dtype) for o in outs),
        in_specs=[vmem] * 5,
        out_specs=(anywhere,) * 5,
        scratch_shapes=[pltpu.SemaphoreType.DMA((5,))],
    )(*(pltpu.with_memory_space_constraint(o, pltpu.VMEM) for o in outs))
    return (attended[None], grad_q[None], grad_k[None], grad_v[None], bias_grad)


def solution(mesh):
    rows = P("dp", "ctx", None)
    return jax.shard_map(
        shards,
        mesh=mesh,
        in_specs=(rows, rows, rows, rows, P(), P("dp", None)),
        out_specs=(rows, rows, rows, rows, P()),
        check_vma=False,
    )
```

```python
import math

import jax
import jax.numpy as jnp
import numpy as np
from jax import lax
from jax.experimental import pallas as pl
from jax.experimental.pallas import tpu as pltpu
from jax.sharding import PartitionSpec as P

HD = 128
ROWS = 128
SIDE = 4
NEAR = 4
WINDOW = 10
SLOTS = 13
PAIRS = WINDOW // 2
THETA = 1000000.0
FILL = -1e30
MESH = pl.DeviceIdType.MESH
F32 = jnp.float32
BF16 = jnp.bfloat16


def bias_stages(dp_size):
    if dp_size == 32:
        return [("z", 4 * SIDE), ("x", SIDE), ("yc", 2 * SIDE)]
    return [("z", SIDE), ("x", SIDE)]


def need(dr, reader, col):
    if dr == 0:
        return col < reader
    if dr == 1:
        return col >= 0
    return col >= reader - 1


def kernel(
    dp_size, group, q_hbm, k_hbm, v_hbm, do_hbm, bias_ref, len_ref, freq_ref,
    att_ref, gq_ref, gk_ref, gv_ref, bg_ref,
    q_ref, k_ref, v_ref, do_ref,
    kbuf, vbuf, qs, dos, s_ref, p_ref, w_ref, ds_ref, acc_ref,
    gkb, gvb, far_k, far_v, nl_k, nl_v, nr_k, nr_v, rz_k, rz_v, zs_k, zs_v, sp_k, sp_v,
    acck, accv, bst, cos_ref, sin_ref, start_ref,
    send_sems, krecv, vrecv, rrecv, brecv, local_sems, relay_sem,
):
    c = lax.axis_index("ctx")
    d = lax.axis_index("dp")
    x = lax.rem(c, SIDE)
    z = lax.div(c, SIDE)
    base = z * SIDE
    xr, xl, xo = lax.rem(x + 1, SIDE), lax.rem(x + 3, SIDE), lax.rem(x + 2, SIDE)
    right, left = base + xr, base + xl
    scale = 1.0 / math.sqrt(HD)
    heads = 2 * group
    special_from, special_to = c == 3, c == 12

    def load(src, dst, i):
        pltpu.make_async_copy(src, dst, local_sems.at[i]).start()

    def loaded(src, dst, i):
        pltpu.make_async_copy(src, dst, local_sems.at[i]).wait()

    barrier = pltpu.get_barrier_semaphore()
    stages = bias_stages(dp_size)

    def peer(kind, size, step):
        if kind == "x":
            other = lax.rem(x + step, SIDE)
            return {"ctx": base + other}, x, other
        if kind == "z":
            high = lax.rem(lax.div(d, 2), SIDE) if size > SIDE else 0
            at = high * SIDE + z
            other = lax.rem(at + step, size)
            ctx = lax.rem(other, SIDE) * SIDE + x
            return {"dp": d + (lax.div(other, SIDE) - high) * 2, "ctx": ctx}, at, other
        y, core = lax.div(d, 8), lax.rem(d, 2)
        at = y * 2 + core
        other = lax.rem(at + step, size)
        move = (lax.div(other, 2) - y) * 8 + lax.rem(other, 2) - core
        return {"dp": d + move}, at, other

    count = jnp.where(special_from | special_to, 1, 0)
    for kind, size in stages:
        greeted = [s for s in range(1, size) if min(s, size - s) <= NEAR or kind != "z"]
        for step in greeted:
            target, _, _ = peer(kind, size, step)
            pl.semaphore_signal(barrier, inc=1, device_id=target, device_id_type=MESH)
        count = count + len(greeted)

    @pl.when(special_from)
    def _():
        pl.semaphore_signal(barrier, inc=1, device_id={"ctx": c + 9}, device_id_type=MESH)

    @pl.when(special_to)
    def _():
        pl.semaphore_signal(barrier, inc=1, device_id={"ctx": c - 9}, device_id_type=MESH)

    load(q_hbm, q_ref, 0)
    load(do_hbm, do_ref, 1)
    load(k_hbm, k_ref, 2)
    load(v_hbm, v_ref, 3)
    pending = []

    def slot(buf, s, blocks=1):
        return buf.at[pl.ds(pl.multiple_of(s * ROWS, ROWS), blocks * ROWS)]

    def send(pred, src, dst, recv_sem, target):
        target = target if isinstance(target, dict) else {"ctx": target}
        copy = pltpu.make_async_remote_copy(
            src_ref=src, dst_ref=dst, send_sem=send_sems.at[len(pending)], recv_sem=recv_sem,
            device_id=target, device_id_type=MESH,
        )
        pending.append((pred, copy))

        @pl.when(pred)
        def _():
            copy.start()

    def arrived(pred, dst, recv_sem):
        copy = pltpu.make_async_remote_copy(
            src_ref=dst, dst_ref=dst, send_sem=send_sems.at[0], recv_sem=recv_sem,
            device_id={"ctx": right}, device_id_type=MESH,
        )

        @pl.when(pred)
        def _():
            copy.wait_recv()

    def first(dr):
        return 9 - SIDE * dr

    def far_path(dr):
        return dr != 2

    def spread(buf, recv, is_key, dr):
        valid = z >= dr
        s = first(dr) + x
        own, sem = slot(buf, s), recv.at[s]
        if dr:
            arrived(valid, own, sem)
        if dr < 2:
            up = slot(buf, s - SIDE)
            send(valid & (z < SIDE - 1), own, up, recv.at[s - SIDE], c + SIDE)
        far = need(dr, xo, x)
        if not far_path(dr):
            send(valid & far, own, own, sem, base + xo)
        to_right, to_left = need(dr, xr, x), need(dr, xl, x)
        on_right, on_left = far_path(dr) & is_key, far_path(dr) & (not is_key)
        send(valid & (to_right | far if on_right else to_right), own, own, sem, right)
        send(valid & (to_left | far if on_left else to_left), own, own, sem, left)
        if dr == 0:
            send(special_from, own, slot(buf, 0), recv.at[0], c + 9)

    def forward_keys(dr):
        valid = z >= dr
        sl, sr = first(dr) + xl, first(dr) + xr
        kl, kr = slot(kbuf, sl), slot(kbuf, sr)
        use_l, use_r = need(dr, x, xl), need(dr, x, xr)
        on = need(dr, xr, xl) & far_path(dr)
        arrived(valid & (use_l | on), kl, krecv.at[sl])
        if far_path(dr):
            send(valid & on, kl, kl, krecv.at[sl], right)
        arrived(valid & use_r, kr, krecv.at[sr])

    def forward_values(dr):
        valid = z >= dr
        sl, sr = first(dr) + xl, first(dr) + xr
        vl, vr = slot(vbuf, sl), slot(vbuf, sr)
        use_l, use_r = need(dr, x, xl), need(dr, x, xr)
        on = need(dr, xl, xr) & far_path(dr)
        arrived(valid & (use_r | on), vr, vrecv.at[sr])
        if far_path(dr):
            send(valid & on, vr, vr, vrecv.at[sr], left)
        arrived(valid & use_l, vl, vrecv.at[sl])

    def last(buf, recv):
        for dr in (0, 1, 2):
            so = first(dr) + xo
            arrived((z >= dr) & need(dr, x, xo), slot(buf, so), recv.at[so])

    pos = c * ROWS + lax.broadcasted_iota(jnp.int32, (ROWS, HD), 0)
    start = jnp.zeros((ROWS, HD), jnp.int32)
    end = jnp.int32(0)
    for i in range(len_ref.shape[1]):
        length = len_ref[0, i]
        end = end + length
        start = start + jnp.where(end <= pos, length, 0)
    start_ref[...] = start
    angle = (pos - start).astype(F32) * freq_ref[...]
    lane = lax.broadcasted_iota(jnp.int32, (ROWS, HD), 1)
    cos_ref[...] = jnp.cos(angle)
    sine = jnp.sin(angle)
    sin_ref[...] = jnp.where(lane < HD // 2, -sine, sine)

    def rope(value):
        return value * cos_ref[...] + pltpu.roll(value, HD // 2, 1) * sin_ref[...]

    def rope_back(value):
        return value * cos_ref[...] - pltpu.roll(value, HD // 2, 1) * sin_ref[...]

    loaded(k_hbm, k_ref, 2)
    own_rows = pl.ds(pl.multiple_of((9 + x) * ROWS, ROWS), ROWS)
    for g in range(2):
        cols = slice(g * HD, (g + 1) * HD)
        kbuf[own_rows, cols] = rope(k_ref[:, cols].astype(F32)).astype(BF16)
    loaded(v_hbm, v_ref, 3)
    vbuf[own_rows, :] = v_ref[...]

    def clear(s):
        rows = pl.ds(pl.multiple_of(s * ROWS, ROWS), ROWS)
        kbuf[rows, :] = jnp.zeros((ROWS, 2 * HD), BF16)
        vbuf[rows, :] = jnp.zeros((ROWS, 2 * HD), BF16)

    for dr in (1, 2):

        @pl.when(z < dr)
        def _():
            for i in range(SIDE):
                clear(jnp.int32(first(dr) + i))

    @pl.when(c != 12)
    def _():
        clear(jnp.int32(0))

    @pl.when(x == 0)
    def _():
        gvb[10 * ROWS : 11 * ROWS, :] = jnp.zeros((ROWS, 2 * HD), BF16)

    loaded(q_hbm, q_ref, 0)
    loaded(do_hbm, do_ref, 1)
    for h in range(heads):
        g, r = h // group, (h % group) * ROWS
        cols = slice(h * HD, (h + 1) * HD)
        qs[g, r : r + ROWS, :] = rope(q_ref[:, cols].astype(F32) + bias_ref[cols]).astype(BF16)
        dos[g, r : r + ROWS, :] = do_ref[:, cols]

    nt = (((1,), (1,)), ((), ()))
    tn = (((0,), (0,)), ((), ()))
    nn = (((1,), (0,)), ((), ()))

    def window(p):
        return pl.ds(pl.multiple_of((x + 2 * p) * ROWS, ROWS), 2 * ROWS)

    first_key = (c - (WINDOW - 1)) * ROWS

    def pair_cols(p):
        return pl.ds(pl.multiple_of(p * 2 * ROWS, 2 * ROWS), 2 * ROWS)

    def score_step(p):
        key_pos = first_key + p * 2 * ROWS + lax.broadcasted_iota(jnp.int32, (ROWS, 2 * ROWS), 1)
        row = c * ROWS + lax.broadcasted_iota(jnp.int32, (ROWS, 2 * ROWS), 0)
        begin = jnp.concatenate([start_ref[...], start_ref[...]], axis=1)
        visible = (key_pos <= row) & (key_pos >= begin)
        for g in range(2):
            keys = kbuf[window(p), g * HD : (g + 1) * HD]
            raw = lax.dot_general(qs[g], keys, nt, preferred_element_type=F32)
            for h in range(group):
                rows = slice(h * ROWS, (h + 1) * ROWS)
                s_ref[g, rows, pair_cols(p)] = jnp.where(visible, raw[rows], FILL)
        return 0

    def prob_step(p):
        for g in range(2):
            values = vbuf[window(p), g * HD : (g + 1) * HD]
            p_ref[g, :, pair_cols(p)] = lax.dot_general(
                dos[g], values, nt, preferred_element_type=F32
            )
        return 0

    pl.semaphore_wait(barrier, count)
    kind, size = stages[0]
    relayed = size > 2 * NEAR
    if relayed:
        for step in (NEAR, size - NEAR):
            target, _, _ = peer(kind, size, step)
            pl.semaphore_signal(relay_sem, inc=1, device_id=target, device_id_type=MESH)
    spread(kbuf, krecv, True, 0)
    spread(vbuf, vrecv, False, 0)
    spread(kbuf, krecv, True, 1)
    forward_keys(0)
    spread(vbuf, vrecv, False, 1)
    forward_values(0)
    spread(kbuf, krecv, True, 2)
    forward_keys(1)
    spread(vbuf, vrecv, False, 2)
    forward_values(1)
    score_step(4)
    forward_keys(2)
    arrived(special_to, slot(kbuf, 0), krecv.at[0])
    lax.fori_loop(0, 2, lambda i, carry: score_step(2 - 2 * i), 0)
    prob_step(4)
    last(kbuf, krecv)
    lax.fori_loop(0, 2, lambda i, carry: score_step(3 - 2 * i), 0)

    factor = scale * math.log2(math.e)

    whole = pl.ds(pl.multiple_of(x * ROWS, ROWS), WINDOW * ROWS)
    chunk = ROWS // 4

    def softmax_step(h, carry):
        for g in range(2):
            for r in range(4):
                rows = pl.ds(pl.multiple_of(h * ROWS, ROWS) + r * chunk, chunk)
                scores = s_ref[g, rows, :]
                top = jnp.max(scores, axis=1, keepdims=True)
                terms = jnp.exp2((scores - top) * factor)
                total = jnp.sum(terms, axis=1, keepdims=True)
                w_ref[g, rows, :] = (terms * (1.0 / total)).astype(BF16)
        return carry

    lax.fori_loop(0, group, softmax_step, 0)
    forward_values(2)
    arrived(special_to, slot(vbuf, 0), vrecv.at[0])
    last(vbuf, vrecv)
    lax.fori_loop(0, PAIRS - 1, lambda p, carry: prob_step(p), 0)
    for g in range(2):
        values = vbuf[whole, g * HD : (g + 1) * HD]
        acc_ref[g] = lax.dot_general(w_ref[g], values, nn, preferred_element_type=F32)

    _, at_0, _ = peer(*stages[0], 1)

    def dscore_step(h, carry):
        for g in range(2):
            cols = pl.ds(pl.multiple_of((g * group + h) * HD, HD), HD)
            for r in range(4):
                rows = pl.ds(pl.multiple_of(h * ROWS, ROWS) + r * chunk, chunk)
                attended = acc_ref[g, rows, :].astype(BF16)
                att_ref[r * chunk : (r + 1) * chunk, cols] = attended
                product = dos[g, rows, :].astype(F32) * attended.astype(F32)
                delta = jnp.sum(product, axis=1, keepdims=True)
                weights = w_ref[g, rows, :].astype(F32)
                ds_ref[g, rows, :] = (weights * (p_ref[g, rows, :] - delta)).astype(BF16)
        return carry

    lax.fori_loop(0, group, dscore_step, 0)
    def bias_start(i):
        kind, size = stages[i]
        for step in range(1, size):
            target, at, _ = peer(kind, size, step)
            send(c >= 0, bst.at[i, at], bst.at[i, at], brecv.at[i, at], target)

    def bias_end(i):
        kind, size = stages[i]
        for step in range(1, size):
            _, _, other = peer(kind, size, step)
            arrived(c >= 0, bst.at[i, other], brecv.at[i, other])
        total = bst[i, 0]
        for j in range(1, size):
            total = total + bst[i, j]
        if i + 1 < len(stages):
            _, at, _ = peer(*stages[i + 1], 1)
            bst[i + 1, at] = total
            bias_start(i + 1)
        else:
            total = total * (1.0 / math.sqrt(dp_size * SIDE * SIDE * ROWS))
            for h in range(heads):
                bg_ref[h * HD : (h + 1) * HD] = total[h]

    def term_step(p, carry):
        for g in range(2):
            cols = slice(g * HD, (g + 1) * HD)
            key_term = lax.dot_general(
                ds_ref[g, :, pair_cols(p)], qs[g], tn, preferred_element_type=F32
            )
            value_term = lax.dot_general(
                w_ref[g, :, pair_cols(p)], dos[g], tn, preferred_element_type=F32
            )
            gkb[window(p), cols] = (scale * key_term).astype(BF16)
            gvb[window(p), cols] = value_term.astype(BF16)
        return carry

    def back_far(dr):
        so = first(dr) + xo
        pred = (z >= dr) & need(dr, x, xo)
        to_k, to_v = (left, right) if far_path(dr) else (base + xo, base + xo)
        send(pred, slot(gkb, so), far_k.at[dr], rrecv.at[dr, 0], to_k)
        send(pred, slot(gvb, so), far_v.at[dr], rrecv.at[dr, 1], to_v)
        valid = z >= dr
        to_l, to_r = valid & need(dr, x, xl), valid & need(dr, x, xr)
        send(to_l, slot(gvb, first(dr) + xl), nr_v.at[dr], rrecv.at[dr, 3], left)
        send(to_r, slot(gkb, first(dr) + xr), nl_k.at[dr], rrecv.at[dr, 4], right)

    def add_into(buf, s, other):
        rows = pl.ds(pl.multiple_of(s * ROWS, ROWS), ROWS)
        buf[rows, :] = (buf[rows, :].astype(F32) + other[...].astype(F32)).astype(BF16)

    def back_near(dr):
        valid = z >= dr
        sl, sr = first(dr) + xl, first(dr) + xr
        to_l, to_r = valid & need(dr, x, xl), valid & need(dr, x, xr)
        if not far_path(dr):
            send(to_l, slot(gkb, sl), nr_k.at[dr], rrecv.at[dr, 2], left)
            send(to_r, slot(gvb, sr), nl_v.at[dr], rrecv.at[dr, 5], right)
            return
        got = valid & need(dr, xr, xl)
        arrived(got, far_k.at[dr], rrecv.at[dr, 0])

        @pl.when(got)
        def _():
            add_into(gkb, sl, far_k.at[dr])

        send(to_l | got, slot(gkb, sl), nr_k.at[dr], rrecv.at[dr, 2], left)
        got_v = valid & need(dr, xl, xr)
        arrived(got_v, far_v.at[dr], rrecv.at[dr, 1])

        @pl.when(got_v)
        def _():
            add_into(gvb, sr, far_v.at[dr])

        send(to_r | got_v, slot(gvb, sr), nl_v.at[dr], rrecv.at[dr, 5], right)

    def add_when(pred, acc, src, sem):
        arrived(pred, src, sem)

        @pl.when(pred)
        def _():
            acc[...] += src[...].astype(F32)

    def back_sum(dr):
        valid = z >= dr
        so = pl.ds(pl.multiple_of((first(dr) + x) * ROWS, ROWS), ROWS)
        acck[...] = gkb[so, :].astype(F32)
        accv[...] = gvb[so, :].astype(F32)
        near_l, near_r, far = need(dr, xl, x), need(dr, xr, x), need(dr, xo, x)
        add_when(valid & near_r, accv, nr_v.at[dr], rrecv.at[dr, 3])
        add_when(valid & near_l, acck, nl_k.at[dr], rrecv.at[dr, 4])
        passed = far & far_path(dr)
        add_when(valid & (near_r | passed), acck, nr_k.at[dr], rrecv.at[dr, 2])
        add_when(valid & (near_l | passed), accv, nl_v.at[dr], rrecv.at[dr, 5])
        if not far_path(dr):
            add_when(valid & far, acck, far_k.at[dr], rrecv.at[dr, 0])
            add_when(valid & far, accv, far_v.at[dr], rrecv.at[dr, 1])
        if dr:
            zs_k[dr - 1] = acck[...].astype(BF16)
            zs_v[dr - 1] = accv[...].astype(BF16)
            down = c - SIDE * dr
            send(valid, zs_k.at[dr - 1], rz_k.at[dr - 1], rrecv.at[dr, 6], down)
            send(valid, zs_v.at[dr - 1], rz_v.at[dr - 1], rrecv.at[dr, 7], down)

    lax.fori_loop(0, 3, term_step, 0)
    back_far(2)
    back_near(2)

    for g in range(2):
        keys = kbuf[whole, g * HD : (g + 1) * HD]
        acc_ref[g] = lax.dot_general(ds_ref[g], keys, nn, preferred_element_type=F32)
    for h in range(heads):
        g, r = h // group, (h % group) * ROWS
        cols = slice(h * HD, (h + 1) * HD)
        before = rope_back(scale * acc_ref[g, r : r + ROWS])
        gq_ref[:, cols] = before.astype(BF16)
        bst[0, at_0, h : h + 1, :] = jnp.sum(before, axis=0, keepdims=True)
    pad = bst.shape[2] - heads
    if pad:
        bst[0, at_0, heads:, :] = jnp.zeros((pad, HD), F32)
    if relayed:
        pl.semaphore_wait(relay_sem, 2)
    bias_start(0)

    lax.fori_loop(3, PAIRS, term_step, 0)
    back_far(1)
    back_far(0)
    send(special_to, slot(gkb, 0), sp_k, rrecv.at[0, 6], c - 9)
    send(special_to, slot(gvb, 0), sp_v, rrecv.at[0, 7], c - 9)
    back_near(1)
    bias_end(0)
    back_near(0)
    back_sum(2)
    back_sum(1)
    if len(stages) > 2:
        bias_end(1)
    back_sum(0)
    for dr in (2, 1):
        add_when(z + dr < SIDE, acck, rz_k.at[dr - 1], rrecv.at[dr, 6])
        add_when(z + dr < SIDE, accv, rz_v.at[dr - 1], rrecv.at[dr, 7])
    add_when(special_from, acck, sp_k, rrecv.at[0, 6])
    add_when(special_from, accv, sp_v, rrecv.at[0, 7])
    for g in range(2):
        cols = slice(g * HD, (g + 1) * HD)
        gk_ref[:, cols] = rope_back(acck[:, cols]).astype(BF16)
    gv_ref[...] = accv[...].astype(BF16)
    bias_end(len(stages) - 1)

    for pred, copy in pending:

        @pl.when(pred)
        def _():
            copy.wait_send()


def write_out(*refs):
    sems = refs[10]
    copies = [pltpu.make_async_copy(refs[i], refs[5 + i], sems.at[i]) for i in range(5)]
    for copy in copies:
        copy.start()
    for copy in copies:
        copy.wait()


def shards(q_lin, k_lin, v_lin, out_grad, q_bias, doc_lengths):
    width = q_lin.shape[2]
    heads = width // HD
    group = heads // 2
    dp_size = lax.axis_size("dp")
    exponent = np.arange(HD // 2, dtype=np.float32) * np.float32(2.0 / HD)
    freq = np.power(np.float32(THETA), -exponent).astype(np.float32)
    freq = jnp.asarray(np.concatenate([freq, freq])[None, :])
    rows = group * ROWS
    anywhere = pl.BlockSpec(memory_space=pl.ANY)
    vmem = pl.BlockSpec(memory_space=pltpu.VMEM)
    block = lambda *lead: pltpu.VMEM((*lead, ROWS, 2 * HD), BF16)
    n_stage = len(bias_stages(dp_size))
    pad_heads = -(-heads // 8) * 8
    outs = pl.pallas_call(
        lambda *refs: kernel(dp_size, group, *refs),
        out_shape=(
            pltpu.VMEM((ROWS, width), BF16),
            pltpu.VMEM((ROWS, width), BF16),
            pltpu.VMEM((ROWS, 2 * HD), BF16),
            pltpu.VMEM((ROWS, 2 * HD), BF16),
            pltpu.VMEM((width,), F32),
        ),
        in_specs=[anywhere] * 4 + [vmem, pl.BlockSpec(memory_space=pltpu.SMEM), vmem],
        out_specs=(vmem,) * 5,
        scratch_shapes=[
            pltpu.VMEM((ROWS, width), BF16), block(), block(), pltpu.VMEM((ROWS, width), BF16),
            pltpu.VMEM((SLOTS * ROWS, 2 * HD), BF16),
            pltpu.VMEM((SLOTS * ROWS, 2 * HD), BF16),
            pltpu.VMEM((2, rows, HD), BF16),
            pltpu.VMEM((2, rows, HD), BF16),
            pltpu.VMEM((2, rows, WINDOW * ROWS), F32),
            pltpu.VMEM((2, rows, WINDOW * ROWS), F32),
            pltpu.VMEM((2, rows, WINDOW * ROWS), BF16),
            pltpu.VMEM((2, rows, WINDOW * ROWS), BF16),
            pltpu.VMEM((2, rows, HD), F32),
            pltpu.VMEM((SLOTS * ROWS, 2 * HD), BF16),
            pltpu.VMEM((SLOTS * ROWS, 2 * HD), BF16),
            block(3), block(3), block(3), block(3), block(3), block(3),
            block(2), block(2), block(2), block(2), block(), block(),
            pltpu.VMEM((ROWS, 2 * HD), F32),
            pltpu.VMEM((ROWS, 2 * HD), F32),
            pltpu.VMEM((n_stage, SIDE * SIDE, pad_heads, HD), F32),
            pltpu.VMEM((ROWS, HD), F32),
            pltpu.VMEM((ROWS, HD), F32),
            pltpu.VMEM((ROWS, HD), jnp.int32),
            pltpu.SemaphoreType.DMA((96,)),
            pltpu.SemaphoreType.DMA((SLOTS,)),
            pltpu.SemaphoreType.DMA((SLOTS,)),
            pltpu.SemaphoreType.DMA((3, 8)),
            pltpu.SemaphoreType.DMA((n_stage, SIDE * SIDE)),
            pltpu.SemaphoreType.DMA((8,)),
            pltpu.SemaphoreType.REGULAR,
        ],
        compiler_params=pltpu.CompilerParams(
            collective_id=0, has_side_effects=True, vmem_limit_bytes=56 * 1024 * 1024
        ),
        cost_estimate=pl.CostEstimate(
            flops=12 * heads * ROWS * WINDOW * ROWS * HD,
            bytes_accessed=4 * 2 * ROWS * width,
            transcendentals=heads * ROWS * WINDOW * ROWS,
        ),
    )(
        q_lin.reshape(ROWS, width), k_lin.reshape(ROWS, 2 * HD), v_lin.reshape(ROWS, 2 * HD),
        out_grad.reshape(ROWS, width), q_bias, doc_lengths, freq,
    )
    attended, grad_q, grad_k, grad_v, bias_grad = pl.pallas_call(
        write_out,
        out_shape=tuple(jax.ShapeDtypeStruct(o.shape, o.dtype) for o in outs),
        in_specs=[vmem] * 5,
        out_specs=(anywhere,) * 5,
        scratch_shapes=[pltpu.SemaphoreType.DMA((5,))],
    )(*(pltpu.with_memory_space_constraint(o, pltpu.VMEM) for o in outs))
    return (attended[None], grad_q[None], grad_k[None], grad_v[None], bias_grad)


def solution(mesh):
    rows = P("dp", "ctx", None)
    return jax.shard_map(
        shards,
        mesh=mesh,
        in_specs=(rows, rows, rows, rows, P(), P("dp", None)),
        out_specs=(rows, rows, rows, rows, P()),
        check_vma=False,
    )
```
